256 devices in a mesh: expert: 32 (over y, x, core), etp: 8 (over z).
Axes of the slice: x: 4, y: 4, z: 8, core: 2. Of those that a mesh axis runs over, the one named last changes fastest.
Arguments:
- tokens: bfloat16 [8192, 2048], P('expert', 'etp'), may hold values from -6 to 6
- expert_ids: int32 [8192, 8], P('expert'), may hold values from 0 to 127, all different within a row; in each aligned block of 256 rows (0 to 255, 256 to 511, ...) at most 24 rows name the same one
- route_weights: float32 [8192, 8], P('expert'), may hold values from 0.05 to 0.3
- gate_weight: bfloat16 [256, 384, 2048], P(('expert', 'etp')), may hold values from -0.125 to 0.125
- up_weight: bfloat16 [256, 384, 2048], P(('expert', 'etp')), may hold values from -0.125 to 0.125
- down_weight: bfloat16 [256, 384, 2048], P(('expert', 'etp')), may hold values from -0.21875 to 0.21875
- grad_out: bfloat16 [8192, 2048], P('expert', 'etp'), may hold values from -6 to 6
Outputs:
- mixed: bfloat16 [8192, 2048], P('expert', 'etp')
- grad_tokens: bfloat16 [8192, 2048], P('expert', 'etp')
- grad_route: float32 [8192, 8], P('expert')
- grad_gate: bfloat16 [256, 384, 2048], P(('expert', 'etp'))
- grad_up: bfloat16 [256, 384, 2048], P(('expert', 'etp'))
- grad_down: bfloat16 [256, 384, 2048], P(('expert', 'etp'))
The draws below stay inside these ranges and needn't reach their ends.
Inputs may be any that keep to these rules, and one draw needn't show every extreme that they name: `expert_ids`: each row names 8 different experts. Among the 256 rows of one index of expert (aligned blocks of rows), no expert is named by more than 24 rows, a bound that some block reaches.
All inputs are finite; a program needn't handle non-finite values.
Results may differ from the reference program's by a relative error of at most 0.0064.
Values may be sent and summed in bfloat16 or wider, within the bound.
No kernel may reach another device: no remote copies, remote signals or barrier semaphores. Data moves between devices by JAX's collectives and lax.ppermute only.
A program may use at most 128 MiB of HBM per device.

```python
import math
import jax
import jax.numpy as jnp
import numpy as np
from jax import lax

D = 2048
FF = 768
TOPK = 8
TOK_DEV = 256
EXPERTS = 128
TOKENS = 8192
CAP = 24
HALVES = 2
FFS = 384
N_EXPERT = 32


def levels(rng, dims, cuts, low, high):
    def one(position, shards_of):
        draws = jax.random.uniform(jax.random.fold_in(jax.random.fold_in(rng, 6), position), (shards_of,), jnp.float32, low / len(cuts), high / len(cuts))
        return jnp.repeat(jnp.exp(draws), dims[position] // shards_of).reshape((-1,) + (1,) * (len(dims) - position - 1))

    factor_of = one(*cuts[0])
    for cut in cuts[1:]:
        factor_of = factor_of * one(*cut)
    return factor_of


def deal_out(key, own, number, rows, amount, top, limit, slope):
    ranking = jax.random.permutation(key, amount)
    heavy_load, common = load_shares(amount, rows * top, limit, slope, True), load_shares(amount, rows * top, limit, slope, False)
    places = jnp.arange(amount)

    def named(lengths, rotation):
        used = int((lengths > 0).sum())
        fixed = max(1, used // 4)
        passed = fixed + (places - fixed + rotation * (used - fixed)) % max(1, amount - fixed)
        return jnp.zeros((amount,), jnp.int32).at[ranking[jnp.where(places < fixed, places, passed)]].set(jnp.asarray(lengths, jnp.int32))

    lengths = jnp.where(number % 4 == 0, named(heavy_load, number // 4), named(common, number - number // 4 - 1))
    mixed = jax.random.permutation(jax.random.fold_in(own, 3), amount)
    source_of, sink = mixed[0:amount // 2 * 2:2], mixed[1:amount // 2 * 2:2]
    margin = jnp.minimum(lengths[source_of] - 1, limit - lengths[sink]) // 2
    margin = jnp.where((source_of == ranking[0]) | (sink == ranking[0]) | (lengths[sink] == 0), 0, jnp.maximum(margin, 0))
    passed = jax.random.randint(jax.random.fold_in(own, 4), (amount // 2,), 0, 1 << 20) % (margin + 1)
    lengths = lengths.at[source_of].add(-passed).at[sink].add(passed)
    items = jnp.searchsorted(jnp.cumsum(lengths), jnp.arange(rows * top), side="right").astype(jnp.int32)
    table = items.reshape(top, rows).T
    table = table[jax.random.permutation(jax.random.fold_in(own, 1), rows)]
    rotation = jax.random.randint(jax.random.fold_in(own, 2), (rows, 1), 0, top)
    return jnp.take_along_axis(table, (jnp.arange(top)[None, :] + rotation) % top, axis=1)


def load_shares(amount, total, bound, slope, full):
    portions = [(1 << 20) // math.isqrt(grade ** slope) + 1 for grade in range(1, amount + 1)]
    largest = bound if full else min(bound, max(-(-total // amount), total * portions[0] // sum(portions)))
    least = 1 if total - largest >= amount - 1 else 0
    given, surplus = [largest] + [least] * (amount - 1), total - largest - least * (amount - 1)
    while surplus > 0:
        candidates = [i for i in range(1, amount) if given[i] < largest] or [i for i in range(1, amount) if given[i] < bound]
        mass, remaining = sum([portions[i] for i in candidates]), surplus
        for i in candidates:
            extra = min(bound - given[i], max(1, remaining * portions[i] // mass), surplus)
            given[i] = given[i] + extra
            surplus = surplus - extra
    return np.array(given)


def bell_draw(rng, dims, spread, limit, cuts=(), kind=jnp.bfloat16):
    entries = jax.random.normal(rng, dims, jnp.float32) * spread
    if len(cuts) > 0:
        entries = levels(rng, dims, cuts, -0.22, 0.18) * entries
    return jnp.clip(entries, min=-limit, max=limit).astype(kind)


def setup_inputs(seed: int = 0) -> dict:
    key_of = jax.random.split(jax.random.key(seed), 8)
    tokens = bell_draw(key_of[0], (TOKENS, D), 1.0, 6.0, ((0, 32), (1, 8)))
    expert_ids_keys = jax.random.split(jax.random.fold_in(key_of[1], 1), TOKENS // TOK_DEV)
    expert_ids_turns = jax.random.permutation(jax.random.fold_in(key_of[1], 3), TOKENS // TOK_DEV)
    expert_ids = jax.vmap(lambda own, number: deal_out(jax.random.fold_in(key_of[1], 2), own, number, TOK_DEV, EXPERTS, TOPK, CAP, 2))(expert_ids_keys, expert_ids_turns).reshape((TOKENS, TOPK))
    route_weights = jnp.clip(0.05 + 0.25 * jax.random.uniform(key_of[2], (TOKENS, TOPK), jnp.float32) ** levels(key_of[2], (TOKENS, TOPK), ((0, 32),), -0.2, 0.2), 0.05, 0.3)
    gate_weight = bell_draw(key_of[3], (EXPERTS * HALVES, FFS, D), D ** -0.5, 0.125, ((0, 256),))
    up_weight = bell_draw(key_of[4], (EXPERTS * HALVES, FFS, D), D ** -0.5, 0.125, ((0, 256),))
    down_weight = bell_draw(key_of[5], (EXPERTS * HALVES, FFS, D), FF ** -0.5, 0.21875, ((0, 256),))
    grad_out = bell_draw(key_of[6], (TOKENS, D), 1.0, 6.0, ((0, 32), (1, 8)))
    return dict(tokens=tokens, expert_ids=expert_ids, route_weights=route_weights, gate_weight=gate_weight, up_weight=up_weight, down_weight=down_weight, grad_out=grad_out)


def expert_pass(inputs):
    expert_in, grad_in, w_gate, w_up, w_down = inputs
    rows_count = expert_in.shape[0]
    gate_act = jnp.dot(expert_in, w_gate.T, preferred_element_type=jnp.float32)
    up_act = jnp.dot(expert_in, w_up.T, preferred_element_type=jnp.float32)
    gate_sig = jax.nn.sigmoid(gate_act)
    hidden = (gate_act * gate_sig * up_act).astype(jnp.bfloat16)
    hidden_blocks = hidden.astype(jnp.float32).reshape(rows_count, HALVES, FFS)
    down_blocks = w_down.astype(jnp.float32).reshape(HALVES, FFS, D)
    partial_value = jnp.einsum("mbf,bfd->bmd", hidden_blocks, down_blocks, precision=lax.Precision.HIGHEST)
    expert_part = partial_value.astype(jnp.bfloat16)
    grad_hidden = jnp.dot(grad_in, w_down.T, preferred_element_type=jnp.float32)
    grad_gate_act = (grad_hidden * up_act * gate_sig * (1.0 + gate_act * (1.0 - gate_sig))).astype(jnp.bfloat16)
    grad_up_act = (grad_hidden * gate_act * gate_sig).astype(jnp.bfloat16)
    grad_down = jnp.dot(hidden.T, grad_in, preferred_element_type=jnp.float32).astype(jnp.bfloat16)
    grad_gate = jnp.dot(grad_gate_act.T, expert_in, preferred_element_type=jnp.float32).astype(jnp.bfloat16)
    grad_up = jnp.dot(grad_up_act.T, expert_in, preferred_element_type=jnp.float32).astype(jnp.bfloat16)
    gate_blocks = w_gate.astype(jnp.float32).reshape(HALVES, FFS, D)
    up_blocks = w_up.astype(jnp.float32).reshape(HALVES, FFS, D)
    input_part = jnp.einsum("mbf,bfd->bmd", grad_gate_act.astype(jnp.float32).reshape(rows_count, HALVES, FFS), gate_blocks, precision=lax.Precision.HIGHEST)
    input_part = input_part + jnp.einsum("mbf,bfd->bmd", grad_up_act.astype(jnp.float32).reshape(rows_count, HALVES, FFS), up_blocks, precision=lax.Precision.HIGHEST)
    input_blocks = input_part.astype(jnp.bfloat16)
    return expert_part, input_blocks, grad_gate, grad_up, grad_down


def reference(tokens, expert_ids, route_weights, gate_weight, up_weight, down_weight, grad_out):
    gate_full = gate_weight.reshape(EXPERTS, FF, D)
    up_full = up_weight.reshape(EXPERTS, FF, D)
    down_full = down_weight.reshape(EXPERTS, FF, D)
    flat_ids = expert_ids.reshape(N_EXPERT, TOK_DEV * TOPK).astype(jnp.int32)
    one_hot = (flat_ids[:, :, None] == jnp.arange(EXPERTS, dtype=jnp.int32)[None, None, :]).astype(jnp.int32)
    rank_rows = jnp.cumsum(one_hot, axis=1) - 1
    slot_index = jnp.sum(rank_rows * one_hot, axis=2).astype(jnp.int32)
    block_ids = jnp.arange(N_EXPERT, dtype=jnp.int32)[:, None]
    target = (flat_ids * (N_EXPERT * CAP) + block_ids * CAP + slot_index).reshape(-1).astype(jnp.int32)
    route_count = TOKENS * TOPK
    source = jnp.full((EXPERTS * N_EXPERT * CAP,), route_count, jnp.int32)
    source = source.at[target].set(jnp.arange(route_count, dtype=jnp.int32))
    padded = jnp.concatenate([tokens, jnp.zeros((1, D), jnp.bfloat16)], axis=0)
    expert_in = padded[source // TOPK].reshape(EXPERTS, N_EXPERT * CAP, D)
    scaled = (route_weights[:, :, None] * grad_out.astype(jnp.float32)[:, None, :]).astype(jnp.bfloat16)
    scaled_pad = jnp.concatenate([scaled.reshape(route_count, D), jnp.zeros((1, D), jnp.bfloat16)], axis=0)
    grad_in = scaled_pad[source].reshape(EXPERTS, N_EXPERT * CAP, D)
    expert_part, input_blocks, grad_gate, grad_up, grad_down = lax.map(
        expert_pass, (expert_in, grad_in, gate_full, up_full, down_full))
    grad_float = grad_out.astype(jnp.float32)
    mixed_sum = jnp.zeros((TOKENS, D), jnp.float32)
    route_sum = jnp.zeros((TOKENS, TOPK), jnp.float32)
    token_sum = jnp.zeros((TOKENS, D), jnp.float32)
    for block in range(HALVES):
        routed = expert_part[:, block].reshape(-1, D)[target].reshape(TOKENS, TOPK, D).astype(jnp.float32)
        mixed_sum = mixed_sum + jnp.sum(route_weights[:, :, None] * routed, axis=1)
        route_sum = route_sum + jnp.sum(grad_float[:, None, :] * routed, axis=2)
        grad_routes = input_blocks[:, block].reshape(-1, D)[target].reshape(TOKENS, TOPK, D).astype(jnp.float32)
        token_sum = token_sum + jnp.sum(grad_routes, axis=1)
    mixed = mixed_sum.astype(jnp.bfloat16)
    grad_tokens = token_sum.astype(jnp.bfloat16)
    grad_gate = grad_gate.reshape(EXPERTS * HALVES, FFS, D)
    grad_up = grad_up.reshape(EXPERTS * HALVES, FFS, D)
    grad_down = grad_down.reshape(EXPERTS * HALVES, FFS, D)
    return mixed, grad_tokens, route_sum, grad_gate, grad_up, grad_down
```

```python
import jax
import jax.numpy as jnp
from jax import lax
from jax.sharding import PartitionSpec as P

EXP_DEV = 4
F32 = jnp.float32
BF16 = jnp.bfloat16


def shift(value, step, lanes):
    return lax.ppermute(value, "etp", [(i, (i + step) % lanes) for i in range(lanes)])


def swap(value, lanes):
    return lax.ppermute(value, "etp", [(i, i ^ 1) for i in range(lanes)])


def dot(a, b, dims):
    return lax.dot_general(a, b, (dims, ((), ())), preferred_element_type=F32)


def across(rows, groups):
    slots, width = rows.shape
    cut = rows.reshape(groups, slots // groups, width)
    moved = lax.all_to_all(cut, "expert", split_axis=0, concat_axis=0, tiled=True)
    return moved.reshape(slots, width)


def per_device(tokens, expert_ids, route_weights, gate_weight, up_weight, down_weight, grad_out):
    tok_count, top_count = expert_ids.shape
    units, model_width = gate_weight.shape[1:]
    shard = tokens.shape[1]
    groups = lax.axis_size("expert")
    lanes = lax.axis_size("etp")
    halves = lanes // EXP_DEV
    experts = EXP_DEV * groups
    capacity = max(2, tok_count * top_count * 3 // (2 * experts))
    slots = groups * capacity
    lane = lax.axis_index("etp")
    local_expert = lane // halves
    parity = lane % halves

    own = [tokens] + [shift(tokens, halves * r, lanes) for r in range(1, EXP_DEV)]
    own = jnp.stack(own)
    tok_half = jnp.concatenate(
        [
            lax.dynamic_index_in_dim(own, (local_expert - j) % EXP_DEV, 0, False)
            for j in range(EXP_DEV)
        ],
        axis=1,
    )

    column = lax.broadcasted_iota(jnp.int32, (1, slots), 1)
    col_expert = column // capacity * EXP_DEV + local_expert
    col_slot = (column % capacity).astype(F32)
    hits = [expert_ids[:, k : k + 1] == col_expert for k in range(top_count)]
    member = hits[0]
    for hit in hits[1:]:
        member = member | hit
    member = member.astype(BF16)
    row = lax.broadcasted_iota(jnp.int32, (tok_count, tok_count), 0)
    earlier = (lax.broadcasted_iota(jnp.int32, (tok_count, tok_count), 1) < row).astype(BF16)
    rank = dot(earlier, member, ((1,), (0,)))
    chosen = (member > 0) & (rank == col_slot)
    select = chosen.astype(BF16)
    weight = jnp.zeros((tok_count, slots), F32)
    for k in range(top_count):
        weight = jnp.where(hits[k], route_weights[:, k : k + 1], weight)
    weight = jnp.where(chosen, weight, 0.0)
    slot_weight = jnp.sum(weight, axis=0)[:, None]
    weight_high = lax.reduce_precision(weight, 8, 7)
    weight_low = (weight - weight_high).astype(BF16)
    weight_high = weight_high.astype(BF16)

    def halved(matrix):
        parts = matrix.reshape(units, EXP_DEV, halves, shard)
        mine = lax.dynamic_index_in_dim(parts, parity, 2, False)
        other = lax.dynamic_index_in_dim(parts, 1 - parity, 2, False)
        return mine.reshape(units, -1), other.reshape(units, -1)

    def joined(mine, other):
        mine = mine.reshape(units, EXP_DEV, 1, shard)
        other = other.reshape(units, EXP_DEV, 1, shard)
        first = jnp.where(parity == 0, mine, other)
        second = jnp.where(parity == 0, other, mine)
        return jnp.concatenate([first, second], axis=2).reshape(1, units, model_width)

    gate_mine, gate_other = halved(gate_weight[0])
    up_mine, up_other = halved(up_weight[0])
    w_down = down_weight[0]

    sent = dot(select, tok_half, ((0,), (0,))).astype(BF16)
    rows_mine = across(sent, groups)
    rows_other = swap(rows_mine, lanes)

    spread = [grad_out] + [shift(grad_out, r, lanes) for r in range(1, lanes)]
    spread = jnp.stack(spread)
    grad_full = jnp.concatenate(
        [lax.dynamic_index_in_dim(spread, (lane - j) % lanes, 0, False) for j in range(lanes)],
        axis=1,
    )
    scaled = (dot(select, grad_full, ((0,), (0,))) * slot_weight).astype(BF16)
    grad_rows = across(scaled, groups)

    last = ((1,), (1,))
    gate_act = dot(rows_mine, gate_mine, last) + dot(rows_other, gate_other, last)
    up_act = dot(rows_mine, up_mine, last) + dot(rows_other, up_other, last)
    gate_sig = jax.nn.sigmoid(gate_act)
    hidden = (gate_act * gate_sig * up_act).astype(BF16)
    flat = ((1,), (0,))
    expert_part = dot(hidden, w_down, flat).astype(BF16)
    returned = across(expert_part, groups)

    grad_hidden = dot(grad_rows, w_down, last)
    grad_gate_act = (
        grad_hidden * up_act * gate_sig * (1.0 + gate_act * (1.0 - gate_sig))
    ).astype(BF16)
    grad_up_act = (grad_hidden * gate_act * gate_sig).astype(BF16)
    input_other = dot(grad_gate_act, gate_other, flat) + dot(grad_up_act, up_other, flat)
    input_swapped = swap(input_other.astype(BF16), lanes)
    input_mine = dot(grad_gate_act, gate_mine, flat) + dot(grad_up_act, up_mine, flat)
    input_half = (input_mine + input_swapped.astype(F32)).astype(BF16)
    grad_back = across(input_half, groups)

    tall = ((0,), (0,))
    grad_down = dot(hidden, grad_rows, tall).astype(BF16)[None]
    grad_gate = joined(
        dot(grad_gate_act, rows_mine, tall).astype(BF16),
        dot(grad_gate_act, rows_other, tall).astype(BF16),
    )
    grad_up = joined(
        dot(grad_up_act, rows_mine, tall).astype(BF16),
        dot(grad_up_act, rows_other, tall).astype(BF16),
    )

    mixed_part = dot(weight_high, returned, flat) + dot(weight_low, returned, flat)
    products = jnp.where(chosen, dot(grad_full, returned, last), 0.0)
    route_part = jnp.stack(
        [jnp.sum(jnp.where(hits[k], products, 0.0), axis=1) for k in range(top_count)]
    )
    route_1 = lax.reduce_precision(route_part, 8, 7)
    rest = route_part - route_1
    route_2 = lax.reduce_precision(rest, 8, 7)
    route_3 = rest - route_2
    route_pack = jnp.concatenate([route_1, route_2, route_3], axis=0).astype(BF16)
    route_pack = jnp.pad(route_pack, ((0, 32 - 3 * top_count), (0, shard - tok_count)))
    cut = mixed_part.reshape(tok_count, lanes, shard)
    mixed = lax.dynamic_index_in_dim(cut, lane, 1, False)
    route_sum = route_part
    for r in range(1, lanes):
        piece = lax.dynamic_index_in_dim(cut, (lane + r) % lanes, 1, False).astype(BF16)
        piece = shift(jnp.concatenate([piece, route_pack], axis=0), r, lanes).astype(F32)
        mixed = mixed + piece[:tok_count]
        got = piece[tok_count:, :tok_count]
        route_sum = route_sum + (
            got[:top_count] + got[top_count : 2 * top_count] + got[2 * top_count : 3 * top_count]
        )
    mixed = mixed.astype(BF16)
    grad_route = route_sum.T

    token_part = dot(select, grad_back, flat).reshape(tok_count, EXP_DEV, shard)
    grad_tokens = lax.dynamic_index_in_dim(token_part, local_expert, 1, False)
    for r in range(1, EXP_DEV):
        piece = lax.dynamic_index_in_dim(token_part, (local_expert + r) % EXP_DEV, 1, False)
        grad_tokens = grad_tokens + shift(piece.astype(BF16), halves * r, lanes).astype(F32)
    grad_tokens = grad_tokens.astype(BF16)
    return (mixed, grad_tokens, grad_route, grad_gate, grad_up, grad_down)


def solution(mesh):
    placed = (
        P("expert", "etp"),
        P("expert", None),
        P("expert", None),
        P(("expert", "etp"), None, None),
        P(("expert", "etp"), None, None),
        P(("expert", "etp"), None, None),
        P("expert", "etp"),
    )
    return jax.shard_map(
        per_device,
        mesh=mesh,
        in_specs=placed,
        out_specs=(
            P("expert", "etp"),
            P("expert", "etp"),
            P("expert", None),
            P(("expert", "etp"), None, None),
            P(("expert", "etp"), None, None),
            P(("expert", "etp"), None, None),
        ),
        check_vma=False,
    )
```

```python
import functools

import jax
import jax.numpy as jnp
from jax import lax
from jax.experimental import pallas as pl
from jax.experimental.pallas import tpu as pltpu
from jax.sharding import PartitionSpec as P

EXP_DEV = 4
ROW_CUTS = 3
VMEM_BYTES = 32 * 1024 * 1024
F32 = jnp.float32
BF16 = jnp.bfloat16
LAST = ((1,), (1,))
FLAT = ((1,), (0,))
TALL = ((0,), (0,))


def shift(value, step, lanes):
    return lax.ppermute(value, "etp", [(i, (i + step) % lanes) for i in range(lanes)])


def swap(value, lanes):
    return lax.ppermute(value, "etp", [(i, i ^ 1) for i in range(lanes)])


def dot(a, b, dims):
    return lax.dot_general(a, b, (dims, ((), ())), preferred_element_type=F32)


def across(rows, groups):
    slots, width = rows.shape
    cut = rows.reshape(groups, slots // groups, width)
    moved = lax.all_to_all(cut, "expert", split_axis=0, concat_axis=0, tiled=True)
    return moved.reshape(slots, width)


def call(body, scalars, grid, operands, in_blocks, outs, out_blocks, flops, scratch=()):
    def spec(block):
        return pl.BlockSpec(*block)

    moved = sum(x.size * x.dtype.itemsize for x in (*operands, *outs))
    return pl.pallas_call(
        body,
        grid_spec=pltpu.PrefetchScalarGridSpec(
            num_scalar_prefetch=1,
            grid=grid,
            in_specs=[spec(b) for b in in_blocks],
            out_specs=[spec(b) for b in out_blocks],
            scratch_shapes=list(scratch),
        ),
        out_shape=list(outs),
        compiler_params=pltpu.CompilerParams(vmem_limit_bytes=VMEM_BYTES),
        cost_estimate=pl.CostEstimate(flops=flops, bytes_accessed=moved, transcendentals=0),
    )(scalars, *operands)


def whole(array):
    return (array.shape, lambda i, s: (0,) * array.ndim)


def half_columns(ref, parity, shard, index):
    return ref[:, pl.ds(pl.multiple_of((2 * index + parity) * shard, shard), shard)]


def gather_body(shard, s_ref, select_ref, *refs):
    out_ref = refs[-1]
    local_expert = s_ref[0] // 2
    select = select_ref[...]
    for r, ref in enumerate(refs[:-1]):
        start = pl.multiple_of(lax.rem(local_expert - r + EXP_DEV, EXP_DEV) * shard, shard)
        out_ref[:, pl.ds(start, shard)] = dot(select, ref[...], TALL).astype(BF16)


def first_body(shard, s_ref, rows_ref, gate_ref, up_ref, gate_out, up_out):
    parity = lax.rem(s_ref[0], 2)
    for w_ref, out_ref in ((gate_ref, gate_out), (up_ref, up_out)):
        total = None
        for j in range(EXP_DEV):
            part = dot(
                rows_ref[:, j * shard : (j + 1) * shard],
                half_columns(w_ref, parity, shard, j),
                LAST,
            )
            total = part if total is None else total + part
        out_ref[...] = total


def second_body(
    shard, s_ref, rows_ref, gate_in, up_in, gate_ref, up_ref, down_ref,
    hidden_out, gate_slope, up_slope, part_out,
):
    other = 1 - lax.rem(s_ref[0], 2)
    acts = []
    for w_ref, in_ref in ((gate_ref, gate_in), (up_ref, up_in)):
        total = in_ref[...]
        for j in range(EXP_DEV):
            total = total + dot(
                rows_ref[:, j * shard : (j + 1) * shard],
                half_columns(w_ref, other, shard, j),
                LAST,
            )
        acts.append(total)
    gate_act, up_act = acts
    sig = jax.nn.sigmoid(gate_act)
    gated = gate_act * sig
    hidden = (gated * up_act).astype(BF16)
    hidden_out[...] = hidden
    up_slope[...] = gated
    gate_slope[...] = up_act * sig * (1.0 + gate_act * (1.0 - sig))
    part_out[...] = dot(hidden, down_ref[...], FLAT).astype(BF16)


def third_body(
    shard, s_ref, grad_ref, gate_slope, up_slope, gate_ref, up_ref, down_ref,
    gate_out, up_out, other_out,
):
    other = 1 - lax.rem(s_ref[0], 2)
    grad_hidden = dot(grad_ref[...], down_ref[...], LAST)
    grad_gate = (grad_hidden * gate_slope[...]).astype(BF16)
    grad_up = (grad_hidden * up_slope[...]).astype(BF16)
    gate_out[...] = grad_gate
    up_out[...] = grad_up
    for j in range(EXP_DEV):
        other_out[:, j * shard : (j + 1) * shard] = (
            dot(grad_gate, half_columns(gate_ref, other, shard, j), FLAT)
            + dot(grad_up, half_columns(up_ref, other, shard, j), FLAT)
        ).astype(BF16)


def mine_body(shard, s_ref, grad_gate, grad_up, gate_ref, up_ref, out_ref):
    parity = lax.rem(s_ref[0], 2)
    for j in range(EXP_DEV):
        out_ref[:, j * shard : (j + 1) * shard] = dot(
            grad_gate[...], half_columns(gate_ref, parity, shard, j), FLAT
        ) + dot(grad_up[...], half_columns(up_ref, parity, shard, j), FLAT)


def weights_body(
    s_ref, hidden_ref, grad_gate, grad_up, rows_mine, rows_other, grad_ref,
    gate_out, up_out, down_out,
):
    down_out[0] = dot(hidden_ref[...], grad_ref[...], TALL).astype(BF16)
    here = lax.rem(pl.program_id(0), 2) == lax.rem(s_ref[0], 2)

    def write(rows):
        gate_out[0] = dot(grad_gate[...], rows, TALL).astype(BF16)
        up_out[0] = dot(grad_up[...], rows, TALL).astype(BF16)

    @pl.when(here)
    def _():
        write(rows_mine[...])

    @pl.when(jnp.logical_not(here))
    def _():
        write(rows_other[...])


def mix_body(s_ref, high_ref, low_ref, rows_ref, grad_ref, mine_out, piece_out, product_out):
    step = pl.program_id(0)
    rows = rows_ref[...]
    part = dot(high_ref[...], rows, FLAT) + dot(low_ref[...], rows, FLAT)
    product = dot(grad_ref[...], rows, LAST)

    @pl.when(step == 0)
    def _():
        mine_out[...] = part
        product_out[...] = product

    @pl.when(step > 0)
    def _():
        product_out[...] += product

    piece_out[0] = part.astype(BF16)


def spread_body(s_ref, select_ref, rows_ref, mine_out, piece_out):
    part = dot(select_ref[...], rows_ref[...], FLAT)

    @pl.when(pl.program_id(0) == 0)
    def _():
        mine_out[...] = part

    piece_out[0] = part.astype(BF16)


def per_device(tokens, expert_ids, route_weights, gate_weight, up_weight, down_weight, grad_out):
    tok_count, top_count = expert_ids.shape
    units, model_width = gate_weight.shape[1:]
    shard = tokens.shape[1]
    groups = lax.axis_size("expert")
    lanes = lax.axis_size("etp")
    halves = lanes // EXP_DEV
    experts = EXP_DEV * groups
    capacity = max(2, tok_count * top_count * 3 // (2 * experts))
    slots = groups * capacity
    half = model_width // halves
    lane = lax.axis_index("etp")
    local_expert = lane // halves
    scalars = lane.astype(jnp.int32).reshape(1)
    w_gate = gate_weight[0]
    w_up = up_weight[0]
    w_down = down_weight[0]
    block = slots // ROW_CUTS
    row_grid = (ROW_CUTS,)
    unit_flops = 2 * slots * units * half

    def shape(rows, width, kind=BF16):
        return jax.ShapeDtypeStruct((rows, width), kind)

    def row_block(width):
        return ((block, width), lambda i, s: (i, 0))

    grad_full = lax.all_gather(grad_out, "etp", axis=1, tiled=True)
    own = [tokens] + [shift(tokens, halves * r, lanes) for r in range(1, EXP_DEV)]

    column = lax.broadcasted_iota(jnp.int32, (1, slots), 1)
    col_expert = column // capacity * EXP_DEV + local_expert
    col_slot = (column % capacity).astype(F32)
    hits = [expert_ids[:, k : k + 1] == col_expert for k in range(top_count)]
    member = hits[0]
    for hit in hits[1:]:
        member = member | hit
    member = member.astype(BF16)
    row = lax.broadcasted_iota(jnp.int32, (tok_count, tok_count), 0)
    earlier = (lax.broadcasted_iota(jnp.int32, (tok_count, tok_count), 1) < row).astype(BF16)
    rank = dot(earlier, member, FLAT)
    chosen = (member > 0) & (rank == col_slot)
    select = chosen.astype(BF16)
    weight = jnp.zeros((tok_count, slots), F32)
    for k in range(top_count):
        weight = jnp.where(hits[k], route_weights[:, k : k + 1], weight)
    weight = jnp.where(chosen, weight, 0.0)
    slot_weight = jnp.sum(weight, axis=0)[:, None]
    weight_high = lax.reduce_precision(weight, 8, 7)
    weight_low = (weight - weight_high).astype(BF16)
    weight_high = weight_high.astype(BF16)

    (sent,) = call(
        functools.partial(gather_body, shard), scalars, (1,),
        [select, *own], [whole(select)] + [whole(x) for x in own],
        [shape(slots, half)], [((slots, half), lambda i, s: (0, 0))],
        2 * slots * tok_count * half,
    )
    rows_mine = across(sent, groups)
    rows_other = swap(rows_mine, lanes)

    scaled = (dot(select, grad_full, TALL) * slot_weight).astype(BF16)
    grad_rows = across(scaled, groups)

    f32_rows = shape(slots, units, F32)
    bf16_rows = shape(slots, units)
    unit_block = row_block(units)
    gate_first, up_first = call(
        functools.partial(first_body, shard), scalars, row_grid,
        [rows_mine, w_gate, w_up], [row_block(half), whole(w_gate), whole(w_up)],
        [f32_rows, f32_rows], [unit_block, unit_block], 2 * unit_flops,
    )
    hidden, gate_slope, up_slope, expert_part = call(
        functools.partial(second_body, shard), scalars, row_grid,
        [rows_other, gate_first, up_first, w_gate, w_up, w_down],
        [row_block(half), unit_block, unit_block, whole(w_gate), whole(w_up), whole(w_down)],
        [bf16_rows, f32_rows, f32_rows, shape(slots, model_width)],
        [unit_block, unit_block, unit_block, row_block(model_width)], 4 * unit_flops,
    )
    returned = across(expert_part, groups)

    grad_gate_act, grad_up_act, input_other = call(
        functools.partial(third_body, shard), scalars, row_grid,
        [grad_rows, gate_slope, up_slope, w_gate, w_up, w_down],
        [row_block(model_width), unit_block, unit_block]
        + [whole(w_gate), whole(w_up), whole(w_down)],
        [bf16_rows, bf16_rows, shape(slots, half)],
        [unit_block, unit_block, row_block(half)], 4 * unit_flops,
    )
    input_swapped = swap(input_other, lanes)
    (input_mine,) = call(
        functools.partial(mine_body, shard), scalars, row_grid,
        [grad_gate_act, grad_up_act, w_gate, w_up],
        [unit_block, unit_block, whole(w_gate), whole(w_up)],
        [shape(slots, half, F32)], [row_block(half)], 2 * unit_flops,
    )
    input_half = (input_mine + input_swapped.astype(F32)).astype(BF16)
    grad_back = across(input_half, groups)

    pair_block = ((slots, shard), lambda i, s: (0, i // 2))
    grad_shape = jax.ShapeDtypeStruct((1, units, model_width), BF16)
    grad_block = ((1, units, shard), lambda i, s: (0, 0, i))
    grad_gate, grad_up, grad_down = call(
        weights_body, scalars, (lanes,),
        [hidden, grad_gate_act, grad_up_act, rows_mine, rows_other, grad_rows],
        [whole(hidden), whole(hidden), whole(hidden), pair_block, pair_block]
        + [((slots, shard), lambda i, s: (0, i))],
        [grad_shape] * 3, [grad_block] * 3, 6 * unit_flops,
    )

    def ahead(i, s):
        return (0, lax.rem(s[0] + i, lanes))

    own_block = ((tok_count, shard), lambda i, s: (0, 0))
    mixed, mixed_pieces, products = call(
        mix_body, scalars, (lanes,),
        [weight_high, weight_low, returned, grad_full],
        [whole(weight_high), whole(weight_low)]
        + [((slots, shard), ahead), ((tok_count, shard), ahead)],
        [shape(tok_count, shard, F32), jax.ShapeDtypeStruct((lanes, tok_count, shard), BF16)]
        + [shape(tok_count, slots, F32)],
        [own_block, ((1, tok_count, shard), lambda i, s: (i, 0, 0)), whole(select)],
        6 * tok_count * slots * model_width,
    )
    for r in range(1, lanes):
        mixed = mixed + shift(mixed_pieces[r], r, lanes).astype(F32)
    mixed = mixed.astype(BF16)

    products = jnp.where(chosen, products, 0.0)
    route_sum = jnp.stack(
        [jnp.sum(jnp.where(hits[k], products, 0.0), axis=1) for k in range(top_count)]
    )
    route_sum = route_sum + swap(route_sum, lanes)
    route_1 = lax.reduce_precision(route_sum, 8, 7)
    rest = route_sum - route_1
    route_2 = lax.reduce_precision(rest, 8, 7)
    route_3 = rest - route_2
    route_pack = jnp.concatenate([route_1, route_2, route_3], axis=0).astype(BF16)
    pack_rows = -(-3 * top_count // 16) * 16
    route_pack = jnp.pad(
        route_pack, ((0, pack_rows - 3 * top_count), (0, shard - tok_count))
    )

    grad_tokens, token_pieces = call(
        spread_body, scalars, (EXP_DEV,),
        [select, grad_back],
        [whole(select)]
        + [((slots, shard), lambda i, s: (0, lax.rem(s[0] // 2 + i, EXP_DEV)))],
        [shape(tok_count, shard, F32), jax.ShapeDtypeStruct((EXP_DEV, tok_count, shard), BF16)],
        [own_block, ((1, tok_count, shard), lambda i, s: (i, 0, 0))],
        2 * tok_count * slots * half,
    )
    for r in range(1, EXP_DEV):
        piece = jnp.concatenate([token_pieces[r], route_pack], axis=0)
        piece = shift(piece, halves * r, lanes).astype(F32)
        grad_tokens = grad_tokens + piece[:tok_count]
        got = piece[tok_count:, :tok_count]
        route_sum = route_sum + (
            got[:top_count] + got[top_count : 2 * top_count] + got[2 * top_count : 3 * top_count]
        )
    grad_tokens = grad_tokens.astype(BF16)
    grad_route = route_sum.T
    return (mixed, grad_tokens, grad_route, grad_gate, grad_up, grad_down)


def solution(mesh):
    placed = (
        P("expert", "etp"),
        P("expert", None),
        P("expert", None),
        P(("expert", "etp"), None, None),
        P(("expert", "etp"), None, None),
        P(("expert", "etp"), None, None),
        P("expert", "etp"),
    )
    return jax.shard_map(
        per_device,
        mesh=mesh,
        in_specs=placed,
        out_specs=(
            P("expert", "etp"),
            P("expert", "etp"),
            P("expert", None),
            P(("expert", "etp"), None, None),
            P(("expert", "etp"), None, None),
            P(("expert", "etp"), None, None),
        ),
        check_vma=False,
    )
```

```python
import functools

import jax
import jax.numpy as jnp
from jax import lax
from jax.experimental import pallas as pl
from jax.experimental.pallas import tpu as pltpu
from jax.sharding import PartitionSpec as P

EXP_DEV = 4
ROW_CUTS = 3
SWAP_CUTS = 2
VMEM_BYTES = 63 * 1024 * 1024
F32 = jnp.float32
BF16 = jnp.bfloat16
LAST = ((1,), (1,))
FLAT = ((1,), (0,))
TALL = ((0,), (0,))


def shift(value, step, lanes):
    return lax.ppermute(value, "etp", [(i, (i + step) % lanes) for i in range(lanes)])


def swap(value, lanes):
    return lax.ppermute(value, "etp", [(i, i ^ 1) for i in range(lanes)])


def dot(a, b, dims):
    return lax.dot_general(a, b, (dims, ((), ())), preferred_element_type=F32)


def across(rows, groups):
    slots, width = rows.shape
    cut = rows.reshape(groups, slots // groups, width)
    moved = lax.all_to_all(cut, "expert", split_axis=0, concat_axis=0, tiled=True)
    return moved.reshape(slots, width)


def call(body, scalars, grid, operands, in_blocks, outs, out_blocks, flops, aliases=None):
    def spec(block):
        return block[0] if len(block) == 1 else pl.BlockSpec(*block)

    return pl.pallas_call(
        body,
        grid_spec=pltpu.PrefetchScalarGridSpec(
            num_scalar_prefetch=1,
            grid=grid,
            in_specs=[spec(b) for b in in_blocks],
            out_specs=[spec(b) for b in out_blocks],
        ),
        out_shape=list(outs),
        input_output_aliases=aliases or {},
        compiler_params=pltpu.CompilerParams(vmem_limit_bytes=VMEM_BYTES),
        cost_estimate=pl.CostEstimate(flops=1, bytes_accessed=1, transcendentals=0),
    )(scalars, *operands)


def whole(array):
    return (array.shape, lambda i, s: (0,) * array.ndim)


def columns(parity_of, matrix, shard, halves=2):
    rows = matrix.shape[0]
    blocks = [
        ((rows, shard), lambda i, s, j=j: (0, halves * j + parity_of(s))) for j in range(EXP_DEV)
    ]
    return [matrix] * EXP_DEV, blocks


def mine_of(s):
    return lax.rem(s[0], 2)


def other_of(s):
    return 1 - lax.rem(s[0], 2)


def contract(rows_ref, w_refs):
    shard = w_refs[0].shape[1]
    parts = [
        dot(rows_ref[:, j * shard : (j + 1) * shard], w_ref[...], LAST)
        for j, w_ref in enumerate(w_refs)
    ]
    return sum(parts[1:], parts[0])


def gather_body(shard, s_ref, select_ref, *refs):
    out_ref = refs[-1]
    local_expert = s_ref[0] // 2
    select = select_ref[...]
    for r, ref in enumerate(refs[:-1]):
        start = pl.multiple_of(lax.rem(local_expert - r + EXP_DEV, EXP_DEV) * shard, shard)
        out_ref[:, pl.ds(start, shard)] = dot(select, ref[...], TALL).astype(BF16)


def scaled_body(s_ref, select_ref, grad_ref, weight_ref, out_ref):
    out_ref[...] = (dot(select_ref[...], grad_ref[...], TALL) * weight_ref[...]).astype(BF16)


def first_body(s_ref, rows_ref, *refs):
    gate_out, up_out = refs[-2:]
    gate_out[...] = contract(rows_ref, refs[:EXP_DEV])
    up_out[...] = contract(rows_ref, refs[EXP_DEV:-2])


def second_body(s_ref, rows_ref, gate_in, up_in, down_ref, *refs):
    hidden_out, gate_slope, up_slope, part_out = refs[-4:]
    gate_act = gate_in[...] + contract(rows_ref, refs[:EXP_DEV])
    up_act = up_in[...] + contract(rows_ref, refs[EXP_DEV:-4])
    sig = jax.nn.sigmoid(gate_act)
    gated = gate_act * sig
    hidden = (gated * up_act).astype(BF16)
    hidden_out[...] = hidden
    up_slope[...] = gated
    gate_slope[...] = up_act * sig * (1.0 + gate_act * (1.0 - sig))
    part_out[...] = dot(hidden, down_ref[...], FLAT).astype(BF16)


def third_body(s_ref, grad_ref, gate_slope, up_slope, down_ref, *refs):
    gate_out, up_out, other_out = refs[-3:]
    grad_hidden = dot(grad_ref[...], down_ref[...], LAST)
    grad_gate = (grad_hidden * gate_slope[...]).astype(BF16)
    grad_up = (grad_hidden * up_slope[...]).astype(BF16)
    gate_out[...] = grad_gate
    up_out[...] = grad_up
    shard = refs[0].shape[1]
    for j in range(EXP_DEV):
        other_out[:, j * shard : (j + 1) * shard] = (
            dot(grad_gate, refs[j][...], FLAT) + dot(grad_up, refs[EXP_DEV + j][...], FLAT)
        ).astype(BF16)


def fourth_body(s_ref, grad_gate, grad_up, swapped, *refs):
    out_ref = refs[-1]
    shard = refs[0].shape[1]
    for j in range(EXP_DEV):
        here = slice(j * shard, (j + 1) * shard)
        out_ref[:, here] = (
            dot(grad_gate[...], refs[j][...], FLAT)
            + dot(grad_up[...], refs[EXP_DEV + j][...], FLAT)
            + swapped[:, here].astype(F32)
        ).astype(BF16)


def weights_body(s_ref, *refs):
    hidden, other_ref, mine_ref, grad_ref, gate_out, up_out, down_out = refs[-7:]
    cuts = (len(refs) - 7) // 2
    grad_gate, grad_up = refs[:cuts], refs[cuts : 2 * cuts]
    size = grad_gate[0].shape[0]

    def total(lefts, ref):
        parts = [
            dot(left[...], ref[k * size : (k + 1) * size, :], TALL)
            for k, left in enumerate(lefts)
        ]
        return sum(parts[1:], parts[0]).astype(BF16)

    down_out[0] = dot(hidden[...], grad_ref[...], TALL).astype(BF16)
    here = lax.rem(pl.program_id(0), 2) == lax.rem(s_ref[0], 2)

    @pl.when(here)
    def _():
        gate_out[0] = total(grad_gate, mine_ref)
        up_out[0] = total(grad_up, mine_ref)

    @pl.when(jnp.logical_not(here))
    def _():
        gate_out[0] = total(grad_gate, other_ref)
        up_out[0] = total(grad_up, other_ref)


def mix_body(s_ref, weight_ref, rows_ref, out_ref):
    both = dot(weight_ref[...], rows_ref[...], FLAT)
    tok_count = both.shape[0] // 2
    out_ref[...] = both[:tok_count] + both[tok_count:]


def route_body(s_ref, rows_ref, grad_ref, picked_ref, ids_ref, expert_ref, route_out):
    products = dot(rows_ref[...], grad_ref[...], LAST) * picked_ref[...].astype(F32)
    experts = expert_ref[...]
    for k in range(route_out.shape[0]):
        chosen = jnp.where(ids_ref[k : k + 1, :] == experts, products, 0.0)
        route_out[k : k + 1, :] = jnp.sum(chosen, axis=0, keepdims=True)


def spread_body(s_ref, select_ref, rows_ref, mine_out, piece_out):
    count, tok_count, shard = piece_out.shape
    select = select_ref[...]
    for r in range(count):
        start = pl.multiple_of(lax.rem(s_ref[0] // 2 + r, count) * shard, shard)
        part = dot(select, rows_ref[:, pl.ds(start, shard)], FLAT)
        if r == 0:
            mine_out[...] = part
        piece_out[r] = part.astype(BF16)


def per_device(tokens, expert_ids, route_weights, gate_weight, up_weight, down_weight, grad_out):
    tok_count, top_count = expert_ids.shape
    units, model_width = gate_weight.shape[1:]
    shard = tokens.shape[1]
    groups = lax.axis_size("expert")
    lanes = lax.axis_size("etp")
    halves = lanes // EXP_DEV
    experts = EXP_DEV * groups
    capacity = max(2, tok_count * top_count * 3 // (2 * experts))
    slots = groups * capacity
    half = model_width // halves
    lane = lax.axis_index("etp")
    local_expert = lane // halves
    scalars = lane.astype(jnp.int32).reshape(1)
    w_gate = gate_weight[0]
    w_up = up_weight[0]
    w_down = down_weight[0]
    block = slots // ROW_CUTS
    unit_flops = 2 * slots * units * half

    def shape(rows, width, kind=BF16):
        return jax.ShapeDtypeStruct((rows, width), kind)

    def row_block(width, k=None):
        return ((block, width), lambda i, s: (i if k is None else k, 0))

    grad_full = lax.all_gather(grad_out, "etp", axis=1, tiled=True)
    own = [tokens] + [shift(tokens, halves * r, lanes) for r in range(1, EXP_DEV)]

    column = lax.broadcasted_iota(jnp.int32, (1, slots), 1)
    col_expert = column // capacity * EXP_DEV + local_expert
    col_slot = (column % capacity).astype(F32)
    hits = [expert_ids[:, k : k + 1] == col_expert for k in range(top_count)]
    member = hits[0]
    for hit in hits[1:]:
        member = member | hit
    member = member.astype(BF16)
    row = lax.broadcasted_iota(jnp.int32, (tok_count, tok_count), 0)
    earlier = (lax.broadcasted_iota(jnp.int32, (tok_count, tok_count), 1) < row).astype(BF16)
    rank = dot(earlier, member, FLAT)
    chosen = (member > 0) & (rank == col_slot)
    select = chosen.astype(BF16)
    weight = jnp.zeros((tok_count, slots), F32)
    for k in range(top_count):
        weight = jnp.where(hits[k], route_weights[:, k : k + 1], weight)
    weight = jnp.where(chosen, weight, 0.0)
    slot_weight = jnp.sum(weight, axis=0)[:, None]
    weight_high = lax.reduce_precision(weight, 8, 7)
    weight_low = (weight - weight_high).astype(BF16)
    weight_high = weight_high.astype(BF16)

    (sent,) = call(
        functools.partial(gather_body, shard), scalars, (1,),
        [select, *own], [whole(select)] + [whole(x) for x in own],
        [shape(slots, half)], [((slots, half), lambda i, s: (0, 0))],
        2 * slots * tok_count * half,
    )
    rows_mine = across(sent, groups)
    rows_other = swap(rows_mine, lanes)

    (scaled,) = call(
        scaled_body, scalars, (ROW_CUTS,),
        [select, grad_full, slot_weight],
        [((tok_count, block), lambda i, s: (0, i)), whole(grad_full), row_block(1)],
        [shape(slots, model_width)], [row_block(model_width)],
        2 * slots * tok_count * model_width,
    )
    grad_rows = across(scaled, groups)

    f32_rows = shape(slots, units, F32)
    unit_block = row_block(units)
    gate_mine, mine_blocks = columns(mine_of, w_gate, shard)
    gate_other, other_blocks = columns(other_of, w_gate, shard)
    weights_mine = gate_mine + [w_up] * EXP_DEV
    weights_other = gate_other + [w_up] * EXP_DEV
    mine_blocks, other_blocks = mine_blocks * 2, other_blocks * 2
    gate_first, up_first = call(
        first_body, scalars, (ROW_CUTS,),
        [rows_mine, *weights_mine], [row_block(half)] + mine_blocks,
        [f32_rows, f32_rows], [unit_block, unit_block], 2 * unit_flops,
    )
    hidden, gate_slope, up_slope, expert_part = call(
        second_body, scalars, (ROW_CUTS,),
        [rows_other, gate_first, up_first, w_down, *weights_other],
        [row_block(half), unit_block, unit_block, whole(w_down)] + other_blocks,
        [shape(slots, units), f32_rows, f32_rows, shape(slots, model_width)],
        [unit_block, unit_block, unit_block, row_block(model_width)], 4 * unit_flops,
    )

    size = slots // SWAP_CUTS
    cut_units = shape(size, units)
    cut_half = shape(size, half)

    def cut_block(width, k):
        return ((size, width), lambda i, s: (k, 0))

    grad_gate_act, grad_up_act, swapped = [], [], []
    for k in range(SWAP_CUTS):
        got = call(
            third_body, scalars, (1,),
            [grad_rows, gate_slope, up_slope, w_down, *weights_other],
            [cut_block(model_width, k), cut_block(units, k), cut_block(units, k)]
            + [whole(w_down)] + other_blocks,
            [cut_units, cut_units, cut_half],
            [whole(cut_units), whole(cut_units), whole(cut_half)],
            4 * unit_flops // SWAP_CUTS,
        )
        grad_gate_act.append(got[0])
        grad_up_act.append(got[1])
        if k == 0:
            expert_part, first = lax.optimization_barrier((expert_part, got[2]))
            swapped.append(swap(first, lanes))
        else:
            swapped.append(swap(got[2], lanes))
    returned = across(expert_part, groups)

    pair_block = ((slots, shard), lambda i, s: (0, i // 2))
    grad_shape = jax.ShapeDtypeStruct((1, units, model_width), BF16)
    grad_block = ((1, units, shard), lambda i, s: (0, 0, i))
    grad_gate, grad_up, grad_down = call(
        weights_body, scalars, (lanes,),
        [*grad_gate_act, *grad_up_act, hidden, rows_other, rows_mine, grad_rows],
        [whole(cut_units)] * (2 * SWAP_CUTS) + [whole(hidden)]
        + [pair_block, pair_block, ((slots, shard), lambda i, s: (0, i))],
        [grad_shape] * 3, [grad_block] * 3, 6 * unit_flops,
    )

    input_half = []
    for k in range(SWAP_CUTS):
        operands = [grad_gate_act[k], grad_up_act[k], swapped[k], *weights_mine]
        blocks = [whole(cut_units), whole(cut_units), whole(cut_half)] + mine_blocks
        outs, out_blocks, aliases = shape(slots, half), cut_block(half, k), None
        if k > 0:
            aliases = {len(operands) + 1: 0}
            operands.append(input_half)
            blocks.append((pl.BlockSpec(memory_space=pl.ANY),))
        (input_half,) = call(
            fourth_body, scalars, (1,), operands, blocks,
            [outs], [out_blocks], 2 * unit_flops // SWAP_CUTS, aliases,
        )
    input_half, returned, grad_gate, grad_up, grad_down = lax.optimization_barrier(
        (input_half, returned, grad_gate, grad_up, grad_down)
    )
    grad_back = across(input_half, groups)

    both_weights = jnp.concatenate([weight_high, weight_low], axis=0)
    picked = select.T
    ids = expert_ids.T
    row_expert = col_expert.reshape(slots, 1)
    (mixed_part,) = call(
        mix_body, scalars, (2,), [both_weights, returned],
        [whole(both_weights), ((slots, half), lambda i, s: (0, i))],
        [shape(tok_count, model_width, F32)], [((tok_count, half), lambda i, s: (0, i))],
        4 * tok_count * slots * model_width,
    )
    mixed = lax.psum_scatter(mixed_part, "etp", scatter_dimension=1, tiled=True).astype(BF16)
    route_operands = [returned, grad_full, picked, ids, row_expert]
    (route_sum,) = call(
        route_body, scalars, (1,), route_operands, [whole(x) for x in route_operands],
        [shape(top_count, tok_count, F32)], [whole(ids)],
        2 * tok_count * slots * model_width,
    )
    route_sum = route_sum + swap(route_sum, lanes)
    route_1 = lax.reduce_precision(route_sum, 8, 7)
    rest = route_sum - route_1
    route_2 = lax.reduce_precision(rest, 8, 7)
    route_3 = rest - route_2
    route_pack = jnp.concatenate([route_1, route_2, route_3], axis=0).astype(BF16)
    pack_rows = -(-3 * top_count // 16) * 16
    route_pack = jnp.pad(
        route_pack, ((0, pack_rows - 3 * top_count), (0, shard - tok_count))
    )

    spread_outs = [
        shape(tok_count, shard, F32),
        jax.ShapeDtypeStruct((EXP_DEV, tok_count, shard), BF16),
    ]
    grad_tokens, token_pieces = call(
        spread_body, scalars, (1,), [select, grad_back], [whole(select), whole(grad_back)],
        spread_outs, [whole(x) for x in spread_outs], 2 * tok_count * slots * half,
    )
    pieces = [
        shift(jnp.concatenate([token_pieces[r], route_pack], axis=0), halves * r, lanes)
        for r in range(1, EXP_DEV)
    ]
    for piece in pieces:
        piece = piece.astype(F32)
        grad_tokens = grad_tokens + piece[:tok_count]
        got = piece[tok_count:, :tok_count]
        route_sum = route_sum + (
            got[:top_count] + got[top_count : 2 * top_count] + got[2 * top_count : 3 * top_count]
        )
    grad_tokens = grad_tokens.astype(BF16)
    grad_route = route_sum.T
    return (mixed, grad_tokens, grad_route, grad_gate, grad_up, grad_down)


def solution(mesh):
    placed = (
        P("expert", "etp"),
        P("expert", None),
        P("expert", None),
        P(("expert", "etp"), None, None),
        P(("expert", "etp"), None, None),
        P(("expert", "etp"), None, None),
        P("expert", "etp"),
    )
    return jax.shard_map(
        per_device,
        mesh=mesh,
        in_specs=placed,
        out_specs=(
            P("expert", "etp"),
            P("expert", "etp"),
            P("expert", None),
            P(("expert", "etp"), None, None),
            P(("expert", "etp"), None, None),
            P(("expert", "etp"), None, None),
        ),
        check_vma=False,
    )
```

```python
import functools

import jax
import jax.numpy as jnp
from jax import lax
from jax.experimental import pallas as pl
from jax.experimental.pallas import tpu as pltpu
from jax.sharding import PartitionSpec as P

EXP_DEV = 4
ROW_CUTS = 2
SWAP_CUTS = 2
VMEM_BYTES = 28 * 1024 * 1024
F32 = jnp.float32
BF16 = jnp.bfloat16
LAST = ((1,), (1,))
FLAT = ((1,), (0,))
TALL = ((0,), (0,))


def shift(value, step, lanes):
    return lax.ppermute(value, "etp", [(i, (i + step) % lanes) for i in range(lanes)])


def swap(value, lanes):
    return lax.ppermute(value, "etp", [(i, i ^ 1) for i in range(lanes)])


def dot(a, b, dims):
    return lax.dot_general(a, b, (dims, ((), ())), preferred_element_type=F32)


def across(rows, groups):
    slots, width = rows.shape
    cut = rows.reshape(groups, slots // groups, width)
    moved = lax.all_to_all(cut, "expert", split_axis=0, concat_axis=0, tiled=True)
    return moved.reshape(slots, width)


def in_hbm(operand):
    return pltpu.with_memory_space_constraint(operand, pltpu.HBM)


def call(body, scalars, grid, operands, in_blocks, outs, out_blocks, flops, aliases=None, near=()):
    def spec(block):
        return block[0] if len(block) == 1 else pl.BlockSpec(*block)

    operands = [x if any(x is n for n in near) else in_hbm(x) for x in operands]
    return pl.pallas_call(
        body,
        grid_spec=pltpu.PrefetchScalarGridSpec(
            num_scalar_prefetch=1,
            grid=grid,
            in_specs=[spec(b) for b in in_blocks],
            out_specs=[spec(b) for b in out_blocks],
        ),
        out_shape=[pltpu.HBM(x.shape, x.dtype) for x in outs],
        input_output_aliases=aliases or {},
        compiler_params=pltpu.CompilerParams(vmem_limit_bytes=VMEM_BYTES),
        cost_estimate=pl.CostEstimate(flops=1, bytes_accessed=1, transcendentals=0),
    )(scalars, *operands)


def whole(array):
    return (array.shape, lambda i, s: (0,) * array.ndim)


def columns(parity_of, matrix, shard, halves=2):
    rows = matrix.shape[0]
    blocks = [
        ((rows, shard), lambda i, s, j=j: (0, halves * j + parity_of(s))) for j in range(EXP_DEV)
    ]
    return [matrix] * EXP_DEV, blocks


def mine_of(s):
    return lax.rem(s[0], 2)


def other_of(s):
    return 1 - lax.rem(s[0], 2)


def contract(rows_ref, w_refs):
    shard = w_refs[0].shape[1]
    parts = [
        dot(rows_ref[:, j * shard : (j + 1) * shard], w_ref[...], LAST)
        for j, w_ref in enumerate(w_refs)
    ]
    return sum(parts[1:], parts[0])


def gather_body(shard, s_ref, select_ref, *refs):
    out_ref = refs[-1]
    local_expert = s_ref[0] // 2
    select = select_ref[...]
    for r, ref in enumerate(refs[:-1]):
        start = pl.multiple_of(lax.rem(local_expert - r + EXP_DEV, EXP_DEV) * shard, shard)
        out_ref[:, pl.ds(start, shard)] = dot(select, ref[...], TALL).astype(BF16)


def scaled_body(s_ref, select_ref, grad_ref, weight_ref, out_ref):
    out_ref[...] = (dot(select_ref[...], grad_ref[...], TALL) * weight_ref[...]).astype(BF16)


def first_body(s_ref, rows_ref, *refs):
    gate_out, up_out = refs[-2:]
    gate_out[...] = contract(rows_ref, refs[:EXP_DEV])
    up_out[...] = contract(rows_ref, refs[EXP_DEV:-2])


def second_body(s_ref, rows_ref, gate_in, up_in, down_ref, *refs):
    hidden_out, gate_slope, up_slope, part_out = refs[-4:]
    gate_act = gate_in[...] + contract(rows_ref, refs[:EXP_DEV])
    up_act = up_in[...] + contract(rows_ref, refs[EXP_DEV : 2 * EXP_DEV])
    sig = jax.nn.sigmoid(gate_act)
    gated = gate_act * sig
    hidden = (gated * up_act).astype(BF16)
    hidden_out[...] = hidden
    up_slope[...] = gated
    gate_slope[...] = up_act * sig * (1.0 + gate_act * (1.0 - sig))
    part_out[...] = dot(hidden, down_ref[...], FLAT).astype(BF16)


def third_body(s_ref, grad_ref, gate_slope, up_slope, down_ref, *refs):
    gate_out, up_out, other_out = refs[-3:]
    grad_hidden = dot(grad_ref[...], down_ref[...], LAST)
    grad_gate = (grad_hidden * gate_slope[...]).astype(BF16)
    grad_up = (grad_hidden * up_slope[...]).astype(BF16)
    gate_out[...] = grad_gate
    up_out[...] = grad_up
    shard = refs[0].shape[1]
    for j in range(EXP_DEV):
        other_out[:, j * shard : (j + 1) * shard] = (
            dot(grad_gate, refs[j][...], FLAT) + dot(grad_up, refs[EXP_DEV + j][...], FLAT)
        ).astype(BF16)


def fourth_body(s_ref, grad_gate, grad_up, swapped, *refs):
    out_ref = refs[-1]
    shard = refs[0].shape[1]
    for j in range(EXP_DEV):
        here = slice(j * shard, (j + 1) * shard)
        out_ref[:, here] = (
            dot(grad_gate[...], refs[j][...], FLAT)
            + dot(grad_up[...], refs[EXP_DEV + j][...], FLAT)
            + swapped[:, here].astype(F32)
        ).astype(BF16)


def weights_body(s_ref, *refs):
    mine_ref, grad_ref, gate_out, up_out, down_out = refs[-5:]
    cuts = (len(refs) - 5) // 4
    grad_gate, grad_up, hidden, other = (refs[i * cuts : (i + 1) * cuts] for i in range(4))
    size = hidden[0].shape[0]

    def total(lefts, rights):
        parts = [dot(left[...], right, TALL) for left, right in zip(lefts, rights)]
        return sum(parts[1:], parts[0]).astype(BF16)

    def split(ref):
        return [ref[k * size : (k + 1) * size, :] for k in range(cuts)]

    down_out[0] = total(hidden, split(grad_ref))
    here = lax.rem(pl.program_id(0), 2) == lax.rem(s_ref[0], 2)

    @pl.when(here)
    def _():
        rows = split(mine_ref)
        gate_out[0] = total(grad_gate, rows)
        up_out[0] = total(grad_up, rows)

    @pl.when(jnp.logical_not(here))
    def _():
        rows = [ref[...] for ref in other]
        gate_out[0] = total(grad_gate, rows)
        up_out[0] = total(grad_up, rows)


def mix_body(s_ref, weight_ref, rows_ref, out_ref):
    both = dot(weight_ref[...], rows_ref[...], FLAT)
    tok_count = both.shape[0] // 2
    out_ref[...] = both[:tok_count] + both[tok_count:]


def route_body(s_ref, rows_ref, grad_ref, picked_ref, ids_ref, expert_ref, route_out):
    products = dot(rows_ref[...], grad_ref[...], LAST) * picked_ref[...].astype(F32)
    experts = expert_ref[...]
    for k in range(route_out.shape[0]):
        chosen = jnp.where(ids_ref[k : k + 1, :] == experts, products, 0.0)
        route_out[k : k + 1, :] = jnp.sum(chosen, axis=0, keepdims=True)


def spread_body(s_ref, select_ref, rows_ref, pack_ref, mine_out, *outs):
    count, shard = len(outs) + 1, outs[0].shape[1]
    select = select_ref[...]
    tok_count = select.shape[0]
    for r in range(count):
        start = pl.multiple_of(lax.rem(s_ref[0] // 2 + r, count) * shard, shard)
        part = dot(select, rows_ref[:, pl.ds(start, shard)], FLAT)
        if r == 0:
            mine_out[...] = part
        else:
            outs[r - 1][:tok_count, :] = part.astype(BF16)
            outs[r - 1][tok_count:, :] = pack_ref[...]


def per_device(tokens, expert_ids, route_weights, gate_weight, up_weight, down_weight, grad_out):
    tok_count, top_count = expert_ids.shape
    units, model_width = gate_weight.shape[1:]
    shard = tokens.shape[1]
    groups = lax.axis_size("expert")
    lanes = lax.axis_size("etp")
    halves = lanes // EXP_DEV
    experts = EXP_DEV * groups
    capacity = max(2, tok_count * top_count * 3 // (2 * experts))
    slots = groups * capacity
    half = model_width // halves
    lane = lax.axis_index("etp")
    local_expert = lane // halves
    scalars = lane.astype(jnp.int32).reshape(1)
    w_gate = gate_weight[0]
    w_up = up_weight[0]
    w_down = down_weight[0]
    block = slots // ROW_CUTS
    unit_flops = 2 * slots * units * half

    def shape(rows, width, kind=BF16):
        return jax.ShapeDtypeStruct((rows, width), kind)

    def row_block(width, k=None):
        return ((block, width), lambda i, s: (i if k is None else k, 0))

    grad_full = lax.all_gather(grad_out, "etp", axis=1, tiled=True)
    own = [tokens] + [shift(tokens, halves * r, lanes) for r in range(1, EXP_DEV)]

    column = lax.broadcasted_iota(jnp.int32, (1, slots), 1)
    col_expert = column // capacity * EXP_DEV + local_expert
    col_slot = (column % capacity).astype(F32)
    hits = [expert_ids[:, k : k + 1] == col_expert for k in range(top_count)]
    member = hits[0]
    for hit in hits[1:]:
        member = member | hit
    member = member.astype(BF16)
    row = lax.broadcasted_iota(jnp.int32, (tok_count, tok_count), 0)
    earlier = (lax.broadcasted_iota(jnp.int32, (tok_count, tok_count), 1) < row).astype(BF16)
    rank = dot(earlier, member, FLAT)
    chosen = (member > 0) & (rank == col_slot)
    select = chosen.astype(BF16)
    weight = jnp.zeros((tok_count, slots), F32)
    for k in range(top_count):
        weight = jnp.where(hits[k], route_weights[:, k : k + 1], weight)
    weight = jnp.where(chosen, weight, 0.0)
    slot_weight = jnp.sum(weight, axis=0)[:, None]
    weight_high = lax.reduce_precision(weight, 8, 7)
    weight_low = (weight - weight_high).astype(BF16)
    weight_high = weight_high.astype(BF16)

    (sent,) = call(
        functools.partial(gather_body, shard), scalars, (1,),
        [select, *own], [whole(select)] + [whole(x) for x in own],
        [shape(slots, half)], [((slots, half), lambda i, s: (0, 0))],
        2 * slots * tok_count * half,
        near=(select, *own),
    )
    rows_mine = across(sent, groups)
    size = slots // SWAP_CUTS
    rows_other = [swap(rows_mine[k * size : (k + 1) * size], lanes) for k in range(SWAP_CUTS)]

    (scaled,) = call(
        scaled_body, scalars, (ROW_CUTS,),
        [select, grad_full, slot_weight],
        [((tok_count, block), lambda i, s: (0, i)), whole(grad_full), row_block(1)],
        [shape(slots, model_width)], [row_block(model_width)],
        2 * slots * tok_count * model_width,
    )
    grad_rows = across(scaled, groups)

    f32_rows = shape(slots, units, F32)
    unit_block = row_block(units)
    gate_mine, mine_blocks = columns(mine_of, w_gate, shard)
    gate_other, other_blocks = columns(other_of, w_gate, shard)
    weights_mine = gate_mine + [w_up] * EXP_DEV
    weights_other = gate_other + [w_up] * EXP_DEV
    mine_blocks, other_blocks = mine_blocks * 2, other_blocks * 2
    gate_first, up_first = call(
        first_body, scalars, (ROW_CUTS,),
        [rows_mine, *weights_mine], [row_block(half)] + mine_blocks,
        [f32_rows, f32_rows], [unit_block, unit_block], 2 * unit_flops,
        near=(w_gate, w_up, w_down, rows_mine),
    )

    cut_units = shape(size, units)
    cut_wide = shape(size, units, F32)
    cut_half = shape(size, half)

    def cut_block(width, k):
        return ((size, width), lambda i, s: (k, 0))

    def placed(operands, blocks, array, position):
        if array is None:
            return None
        operands.append(array)
        blocks.append((pl.BlockSpec(memory_space=pl.ANY),))
        return {len(operands): position}

    hidden, slopes, expert_part = [], [], None
    for k in range(SWAP_CUTS):
        operands = [rows_other[k], gate_first, up_first, w_down, *weights_other]
        blocks = [whole(cut_half), cut_block(units, k), cut_block(units, k), whole(w_down)]
        blocks = blocks + other_blocks
        aliases = placed(operands, blocks, expert_part, 3)
        got = call(
            second_body, scalars, (1,), operands, blocks,
            [cut_units, cut_wide, cut_wide, shape(slots, model_width)],
            [whole(cut_units), whole(cut_wide), whole(cut_wide), cut_block(model_width, k)],
            4 * unit_flops // SWAP_CUTS, aliases,
            near=(w_gate, w_up, w_down, rows_other[k]),
        )
        hidden.append(got[0])
        slopes.append(got[1:3])
        expert_part = got[3]

    grad_gate_act, grad_up_act, swapped = [], [], []
    for k in range(SWAP_CUTS):
        got = call(
            third_body, scalars, (1,),
            [grad_rows, *slopes[k], w_down, *weights_other],
            [cut_block(model_width, k), whole(cut_wide), whole(cut_wide), whole(w_down)]
            + other_blocks,
            [cut_units, cut_units, cut_half],
            [whole(cut_units), whole(cut_units), whole(cut_half)],
            4 * unit_flops // SWAP_CUTS,
            near=(w_gate, w_up, w_down),
        )
        grad_gate_act.append(got[0])
        grad_up_act.append(got[1])
        swapped.append(swap(got[2], lanes))
    returned = across(expert_part, groups)

    pair_block = ((slots, shard), lambda i, s: (0, i // 2))
    pair_cut = ((size, shard), lambda i, s: (0, i // 2))
    grad_shape = jax.ShapeDtypeStruct((1, units, model_width), BF16)
    grad_block = ((1, units, shard), lambda i, s: (0, 0, i))
    grad_gate, grad_up, grad_down = call(
        weights_body, scalars, (lanes,),
        [*grad_gate_act, *grad_up_act, *hidden, *rows_other, rows_mine, grad_rows],
        [whole(cut_units)] * (3 * SWAP_CUTS) + [pair_cut] * SWAP_CUTS
        + [pair_block, ((slots, shard), lambda i, s: (0, i))],
        [grad_shape] * 3, [grad_block] * 3, 6 * unit_flops,
        near=(rows_mine, *rows_other),
    )

    input_half = []
    for k in range(SWAP_CUTS):
        operands = [grad_gate_act[k], grad_up_act[k], swapped[k], *weights_mine]
        blocks = [whole(cut_units), whole(cut_units), whole(cut_half)] + mine_blocks
        outs, out_blocks, aliases = shape(slots, half), cut_block(half, k), None
        if k > 0:
            aliases = {len(operands) + 1: 0}
            operands.append(input_half)
            blocks.append((pl.BlockSpec(memory_space=pl.ANY),))
        (input_half,) = call(
            fourth_body, scalars, (1,), operands, blocks,
            [outs], [out_blocks], 2 * unit_flops // SWAP_CUTS, aliases,
            near=(w_gate, w_up, w_down, swapped[k]),
        )
    input_half, returned, grad_gate, grad_up, grad_down = lax.optimization_barrier(
        (input_half, returned, grad_gate, grad_up, grad_down)
    )
    grad_back = across(input_half, groups)

    both_weights = jnp.concatenate([weight_high, weight_low], axis=0)
    picked = select.T
    ids = expert_ids.T
    row_expert = col_expert.reshape(slots, 1)
    (mixed_part,) = call(
        mix_body, scalars, (halves,), [both_weights, returned],
        [whole(both_weights), ((slots, half), lambda i, s: (0, i))],
        [shape(tok_count, model_width, F32)],
        [((tok_count, half), lambda i, s: (0, i))],
        4 * tok_count * slots * model_width,
    )
    mixed = lax.psum_scatter(mixed_part, "etp", scatter_dimension=1, tiled=True).astype(BF16)
    route_operands = [returned, grad_full, picked, ids, row_expert]
    (route_sum,) = call(
        route_body, scalars, (1,), route_operands, [whole(x) for x in route_operands],
        [shape(top_count, tok_count, F32)], [whole(ids)],
        2 * tok_count * slots * model_width,
    )
    route_sum = route_sum + swap(route_sum, lanes)
    route_1 = lax.reduce_precision(route_sum, 8, 7)
    rest = route_sum - route_1
    route_2 = lax.reduce_precision(rest, 8, 7)
    route_3 = rest - route_2
    route_pack = jnp.concatenate([route_1, route_2, route_3], axis=0).astype(BF16)
    pack_rows = -(-3 * top_count // 16) * 16
    route_pack = jnp.pad(
        route_pack, ((0, pack_rows - 3 * top_count), (0, shard - tok_count))
    )

    spread_operands = [select, grad_back, route_pack]
    spread_outs = [shape(tok_count, shard, F32)]
    spread_outs += [shape(tok_count + pack_rows, shard)] * (EXP_DEV - 1)
    grad_tokens, *pieces = call(
        spread_body, scalars, (1,), spread_operands, [whole(x) for x in spread_operands],
        spread_outs, [whole(x) for x in spread_outs], 2 * tok_count * slots * half,
        near=(select, grad_back, route_pack),
    )
    pieces = [shift(pieces[r - 1], halves * r, lanes) for r in range(1, EXP_DEV)]
    for piece in pieces:
        piece = piece.astype(F32)
        grad_tokens = grad_tokens + piece[:tok_count]
        got = piece[tok_count:, :tok_count]
        route_sum = route_sum + (
            got[:top_count] + got[top_count : 2 * top_count] + got[2 * top_count : 3 * top_count]
        )
    grad_tokens = grad_tokens.astype(BF16)
    grad_route = route_sum.T
    return (mixed, grad_tokens, grad_route, grad_gate, grad_up, grad_down)


def solution(mesh):
    placed = (
        P("expert", "etp"),
        P("expert", None),
        P("expert", None),
        P(("expert", "etp"), None, None),
        P(("expert", "etp"), None, None),
        P(("expert", "etp"), None, None),
        P("expert", "etp"),
    )
    return jax.shard_map(
        per_device,
        mesh=mesh,
        in_specs=placed,
        out_specs=(
            P("expert", "etp"),
            P("expert", "etp"),
            P("expert", None),
            P(("expert", "etp"), None, None),
            P(("expert", "etp"), None, None),
            P(("expert", "etp"), None, None),
        ),
        check_vma=False,
    )
```

```python
import functools

import jax
import jax.numpy as jnp
from jax import lax
from jax.experimental import pallas as pl
from jax.experimental.pallas import tpu as pltpu
from jax.sharding import PartitionSpec as P

EXP_DEV = 4
ROW_CUTS = 2
SWAP_CUTS = 2
VMEM_BYTES = 28 * 1024 * 1024
F32 = jnp.float32
BF16 = jnp.bfloat16
LAST = ((1,), (1,))
FLAT = ((1,), (0,))
TALL = ((0,), (0,))


def shift(value, step, lanes):
    return lax.ppermute(value, "etp", [(i, (i + step) % lanes) for i in range(lanes)])


def swap(value, lanes):
    return lax.ppermute(value, "etp", [(i, i ^ 1) for i in range(lanes)])


def dot(a, b, dims):
    return lax.dot_general(a, b, (dims, ((), ())), preferred_element_type=F32)


def across(rows, groups):
    slots, width = rows.shape
    cut = rows.reshape(groups, slots // groups, width)
    moved = lax.all_to_all(cut, "expert", split_axis=0, concat_axis=0, tiled=True)
    return moved.reshape(slots, width)


def in_hbm(operand):
    return pltpu.with_memory_space_constraint(operand, pltpu.HBM)


def call(body, scalars, grid, operands, in_blocks, outs, out_blocks, flops, aliases=None, near=()):
    def spec(block):
        return block[0] if len(block) == 1 else pl.BlockSpec(*block)

    operands = [x if any(x is n for n in near) else in_hbm(x) for x in operands]
    return pl.pallas_call(
        body,
        grid_spec=pltpu.PrefetchScalarGridSpec(
            num_scalar_prefetch=1,
            grid=grid,
            in_specs=[spec(b) for b in in_blocks],
            out_specs=[spec(b) for b in out_blocks],
        ),
        out_shape=[pltpu.HBM(x.shape, x.dtype) for x in outs],
        input_output_aliases=aliases or {},
        compiler_params=pltpu.CompilerParams(vmem_limit_bytes=VMEM_BYTES),
        cost_estimate=pl.CostEstimate(flops=1, bytes_accessed=1, transcendentals=0),
    )(scalars, *operands)


def whole(array):
    return (array.shape, lambda i, s: (0,) * array.ndim)


def columns(parity_of, matrix, shard, halves=2):
    rows = matrix.shape[0]
    blocks = [
        ((rows, shard), lambda i, s, j=j: (0, halves * j + parity_of(s))) for j in range(EXP_DEV)
    ]
    return [matrix] * EXP_DEV, blocks


def mine_of(s):
    return lax.rem(s[0], 2)


def other_of(s):
    return 1 - lax.rem(s[0], 2)


def contract(rows_ref, w_refs):
    shard = w_refs[0].shape[1]
    parts = [
        dot(rows_ref[:, j * shard : (j + 1) * shard], w_ref[...], LAST)
        for j, w_ref in enumerate(w_refs)
    ]
    return sum(parts[1:], parts[0])


def gather_body(shard, s_ref, select_ref, *refs):
    out_ref = refs[-1]
    local_expert = s_ref[0] // 2
    select = select_ref[...]
    for r, ref in enumerate(refs[:-1]):
        start = pl.multiple_of(lax.rem(local_expert - r + EXP_DEV, EXP_DEV) * shard, shard)
        out_ref[:, pl.ds(start, shard)] = dot(select, ref[...], TALL).astype(BF16)


def scaled_body(s_ref, select_ref, grad_ref, weight_ref, out_ref):
    out_ref[...] = (dot(select_ref[...], grad_ref[...], TALL) * weight_ref[...]).astype(BF16)


def first_body(s_ref, rows_ref, *refs):
    gate_out, up_out = refs[-2:]
    gate_out[...] = contract(rows_ref, refs[:EXP_DEV])
    up_out[...] = contract(rows_ref, refs[EXP_DEV:-2])


def second_body(s_ref, rows_ref, gate_in, up_in, down_ref, *refs):
    hidden_out, gate_slope, up_slope, part_out = refs[-4:]
    gate_act = gate_in[...] + contract(rows_ref, refs[:EXP_DEV])
    up_act = up_in[...] + contract(rows_ref, refs[EXP_DEV : 2 * EXP_DEV])
    sig = jax.nn.sigmoid(gate_act)
    gated = gate_act * sig
    hidden = (gated * up_act).astype(BF16)
    hidden_out[...] = hidden
    up_slope[...] = gated
    gate_slope[...] = up_act * sig * (1.0 + gate_act * (1.0 - sig))
    part_out[...] = dot(hidden, down_ref[...], FLAT).astype(BF16)


def third_body(s_ref, grad_ref, gate_slope, up_slope, down_ref, *refs):
    gate_out, up_out, other_out = refs[-3:]
    grad_hidden = dot(grad_ref[...], down_ref[...], LAST)
    grad_gate = (grad_hidden * gate_slope[...]).astype(BF16)
    grad_up = (grad_hidden * up_slope[...]).astype(BF16)
    gate_out[...] = grad_gate
    up_out[...] = grad_up
    shard = refs[0].shape[1]
    for j in range(EXP_DEV):
        other_out[:, j * shard : (j + 1) * shard] = (
            dot(grad_gate, refs[j][...], FLAT) + dot(grad_up, refs[EXP_DEV + j][...], FLAT)
        ).astype(BF16)


def fourth_body(s_ref, grad_gate, grad_up, swapped, *refs):
    out_ref = refs[-1]
    shard = refs[0].shape[1]
    for j in range(EXP_DEV):
        here = slice(j * shard, (j + 1) * shard)
        out_ref[:, here] = (
            dot(grad_gate[...], refs[j][...], FLAT)
            + dot(grad_up[...], refs[EXP_DEV + j][...], FLAT)
            + swapped[:, here].astype(F32)
        ).astype(BF16)


def weights_body(s_ref, *refs):
    mine_ref, grad_ref, gate_out, up_out, down_out = refs[-5:]
    cuts = (len(refs) - 5) // 4
    grad_gate, grad_up, hidden, other = (refs[i * cuts : (i + 1) * cuts] for i in range(4))
    size = hidden[0].shape[0]

    def total(lefts, rights):
        parts = [dot(left[...], right, TALL) for left, right in zip(lefts, rights)]
        return sum(parts[1:], parts[0]).astype(BF16)

    def split(ref):
        return [ref[k * size : (k + 1) * size, :] for k in range(cuts)]

    down_out[0] = total(hidden, split(grad_ref))
    here = lax.rem(pl.program_id(0), 2) == lax.rem(s_ref[0], 2)

    @pl.when(here)
    def _():
        rows = split(mine_ref)
        gate_out[0] = total(grad_gate, rows)
        up_out[0] = total(grad_up, rows)

    @pl.when(jnp.logical_not(here))
    def _():
        rows = [ref[...] for ref in other]
        gate_out[0] = total(grad_gate, rows)
        up_out[0] = total(grad_up, rows)


def mix_body(s_ref, weight_ref, rows_ref, out_ref):
    both = dot(weight_ref[...], rows_ref[...], FLAT)
    tok_count = both.shape[0] // 2
    out_ref[...] = both[:tok_count] + both[tok_count:]


def route_body(s_ref, rows_ref, grad_ref, picked_ref, ids_ref, expert_ref, route_out):
    products = dot(rows_ref[...], grad_ref[...], LAST) * picked_ref[...].astype(F32)
    experts = expert_ref[...]
    for k in range(route_out.shape[0]):
        chosen = jnp.where(ids_ref[k : k + 1, :] == experts, products, 0.0)
        route_out[k : k + 1, :] = jnp.sum(chosen, axis=0, keepdims=True)


def spread_body(s_ref, select_ref, rows_ref, pack_ref, mine_out, *outs):
    count, shard = len(outs) + 1, outs[0].shape[1]
    select = select_ref[...]
    tok_count = select.shape[0]
    for r in range(count):
        start = pl.multiple_of(lax.rem(s_ref[0] // 2 + r, count) * shard, shard)
        part = dot(select, rows_ref[:, pl.ds(start, shard)], FLAT)
        if r == 0:
            mine_out[...] = part
        else:
            outs[r - 1][:tok_count, :] = part.astype(BF16)
            outs[r - 1][tok_count:, :] = pack_ref[...]


def per_device(tokens, expert_ids, route_weights, gate_weight, up_weight, down_weight, grad_out):
    tok_count, top_count = expert_ids.shape
    units, model_width = gate_weight.shape[1:]
    shard = tokens.shape[1]
    groups = lax.axis_size("expert")
    lanes = lax.axis_size("etp")
    halves = lanes // EXP_DEV
    experts = EXP_DEV * groups
    capacity = max(2, tok_count * top_count * 3 // (2 * experts))
    slots = groups * capacity
    half = model_width // halves
    lane = lax.axis_index("etp")
    local_expert = lane // halves
    scalars = lane.astype(jnp.int32).reshape(1)
    w_gate = gate_weight[0]
    w_up = up_weight[0]
    w_down = down_weight[0]
    block = slots // ROW_CUTS
    unit_flops = 2 * slots * units * half

    def shape(rows, width, kind=BF16):
        return jax.ShapeDtypeStruct((rows, width), kind)

    def row_block(width, k=None):
        return ((block, width), lambda i, s: (i if k is None else k, 0))

    grad_full = lax.all_gather(grad_out, "etp", axis=1, tiled=True)
    own = [tokens] + [shift(tokens, halves * r, lanes) for r in range(1, EXP_DEV)]

    column = lax.broadcasted_iota(jnp.int32, (1, slots), 1)
    col_expert = column // capacity * EXP_DEV + local_expert
    col_slot = (column % capacity).astype(F32)
    hits = [expert_ids[:, k : k + 1] == col_expert for k in range(top_count)]
    member = hits[0]
    for hit in hits[1:]:
        member = member | hit
    member = member.astype(BF16)
    row = lax.broadcasted_iota(jnp.int32, (tok_count, tok_count), 0)
    earlier = (lax.broadcasted_iota(jnp.int32, (tok_count, tok_count), 1) < row).astype(BF16)
    rank = dot(earlier, member, FLAT)
    chosen = (member > 0) & (rank == col_slot)
    select = chosen.astype(BF16)
    weight = jnp.zeros((tok_count, slots), F32)
    for k in range(top_count):
        weight = jnp.where(hits[k], route_weights[:, k : k + 1], weight)
    weight = jnp.where(chosen, weight, 0.0)
    slot_weight = jnp.sum(weight, axis=0)[:, None]
    weight_high = lax.reduce_precision(weight, 8, 7)
    weight_low = (weight - weight_high).astype(BF16)
    weight_high = weight_high.astype(BF16)

    (sent,) = call(
        functools.partial(gather_body, shard), scalars, (1,),
        [select, *own], [whole(select)] + [whole(x) for x in own],
        [shape(slots, half)], [((slots, half), lambda i, s: (0, 0))],
        2 * slots * tok_count * half,
        near=(select, *own),
    )
    rows_mine = across(sent, groups)
    size = slots // SWAP_CUTS
    rows_other = [swap(rows_mine[k * size : (k + 1) * size], lanes) for k in range(SWAP_CUTS)]

    (scaled,) = call(
        scaled_body, scalars, (ROW_CUTS,),
        [select, grad_full, slot_weight],
        [((tok_count, block), lambda i, s: (0, i)), whole(grad_full), row_block(1)],
        [shape(slots, model_width)], [row_block(model_width)],
        2 * slots * tok_count * model_width,
    )
    grad_rows = across(scaled, groups)

    f32_rows = shape(slots, units, F32)
    unit_block = row_block(units)
    gate_mine, mine_blocks = columns(mine_of, w_gate, shard)
    gate_other, other_blocks = columns(other_of, w_gate, shard)
    weights_mine = gate_mine + [w_up] * EXP_DEV
    weights_other = gate_other + [w_up] * EXP_DEV
    mine_blocks, other_blocks = mine_blocks * 2, other_blocks * 2
    gate_first, up_first = call(
        first_body, scalars, (ROW_CUTS,),
        [rows_mine, *weights_mine], [row_block(half)] + mine_blocks,
        [f32_rows, f32_rows], [unit_block, unit_block], 2 * unit_flops,
        near=(w_gate, w_up, w_down, rows_mine),
    )

    cut_units = shape(size, units)
    cut_wide = shape(size, units, F32)
    cut_half = shape(size, half)

    def cut_block(width, k):
        return ((size, width), lambda i, s: (k, 0))

    def placed(operands, blocks, array, position):
        if array is None:
            return None
        operands.append(array)
        blocks.append((pl.BlockSpec(memory_space=pl.ANY),))
        return {len(operands): position}

    hidden, slopes, expert_part = [], [], None
    for k in range(SWAP_CUTS):
        operands = [rows_other[k], gate_first, up_first, w_down, *weights_other]
        blocks = [whole(cut_half), cut_block(units, k), cut_block(units, k), whole(w_down)]
        blocks = blocks + other_blocks
        aliases = placed(operands, blocks, expert_part, 3)
        got = call(
            second_body, scalars, (1,), operands, blocks,
            [cut_units, cut_wide, cut_wide, shape(slots, model_width)],
            [whole(cut_units), whole(cut_wide), whole(cut_wide), cut_block(model_width, k)],
            4 * unit_flops // SWAP_CUTS, aliases,
            near=(w_gate, w_up, w_down, rows_other[k]),
        )
        hidden.append(got[0])
        slopes.append(got[1:3])
        expert_part = got[3]

    grad_gate_act, grad_up_act, swapped = [], [], []
    for k in range(SWAP_CUTS):
        got = call(
            third_body, scalars, (1,),
            [grad_rows, *slopes[k], w_down, *weights_other],
            [cut_block(model_width, k), whole(cut_wide), whole(cut_wide), whole(w_down)]
            + other_blocks,
            [cut_units, cut_units, cut_half],
            [whole(cut_units), whole(cut_units), whole(cut_half)],
            4 * unit_flops // SWAP_CUTS,
            near=(w_gate, w_up),
        )
        grad_gate_act.append(got[0])
        grad_up_act.append(got[1])
        swapped.append(swap(got[2], lanes))
    returned = across(expert_part, groups)

    pair_block = ((slots, shard), lambda i, s: (0, i // 2))
    pair_cut = ((size, shard), lambda i, s: (0, i // 2))
    grad_shape = jax.ShapeDtypeStruct((1, units, model_width), BF16)
    grad_block = ((1, units, shard), lambda i, s: (0, 0, i))
    grad_gate, grad_up, grad_down = call(
        weights_body, scalars, (lanes,),
        [*grad_gate_act, *grad_up_act, *hidden, *rows_other, rows_mine, grad_rows],
        [whole(cut_units)] * (3 * SWAP_CUTS) + [pair_cut] * SWAP_CUTS
        + [pair_block, ((slots, shard), lambda i, s: (0, i))],
        [grad_shape] * 3, [grad_block] * 3, 6 * unit_flops,
        near=(rows_mine, *rows_other),
    )

    input_half = []
    for k in range(SWAP_CUTS):
        if k == SWAP_CUTS - 1:
            returned, input_half, grad_gate, grad_up, grad_down = lax.optimization_barrier(
                (returned, input_half, grad_gate, grad_up, grad_down)
            )
            both_weights = jnp.concatenate([weight_high, weight_low], axis=0)
            (mixed_part,) = call(
                mix_body, scalars, (halves,), [both_weights, returned],
                [whole(both_weights), ((slots, half), lambda i, s: (0, i))],
                [shape(tok_count, model_width, F32)],
                [((tok_count, half), lambda i, s: (0, i))],
                4 * tok_count * slots * model_width,
            )
            swapped[k], mixed_part = lax.optimization_barrier((swapped[k], mixed_part))
        operands = [grad_gate_act[k], grad_up_act[k], swapped[k], *weights_mine]
        blocks = [whole(cut_units), whole(cut_units), whole(cut_half)] + mine_blocks
        outs, out_blocks, aliases = shape(slots, half), cut_block(half, k), None
        if k > 0:
            aliases = {len(operands) + 1: 0}
            operands.append(input_half)
            blocks.append((pl.BlockSpec(memory_space=pl.ANY),))
        (input_half,) = call(
            fourth_body, scalars, (1,), operands, blocks,
            [outs], [out_blocks], 2 * unit_flops // SWAP_CUTS, aliases,
            near=(w_gate, w_up, w_down, swapped[k]),
        )
    input_half, returned, grad_gate, grad_up, grad_down = lax.optimization_barrier(
        (input_half, returned, grad_gate, grad_up, grad_down)
    )
    grad_back = across(input_half, groups)

    picked = select.T
    ids = expert_ids.T
    row_expert = col_expert.reshape(slots, 1)
    mixed = lax.psum_scatter(mixed_part, "etp", scatter_dimension=1, tiled=True).astype(BF16)
    route_operands = [returned, grad_full, picked, ids, row_expert]
    (route_sum,) = call(
        route_body, scalars, (1,), route_operands, [whole(x) for x in route_operands],
        [shape(top_count, tok_count, F32)], [whole(ids)],
        2 * tok_count * slots * model_width,
    )
    route_sum = route_sum + swap(route_sum, lanes)
    route_1 = lax.reduce_precision(route_sum, 8, 7)
    rest = route_sum - route_1
    route_2 = lax.reduce_precision(rest, 8, 7)
    route_3 = rest - route_2
    route_pack = jnp.concatenate([route_1, route_2, route_3], axis=0).astype(BF16)
    pack_rows = -(-3 * top_count // 16) * 16
    route_pack = jnp.pad(
        route_pack, ((0, pack_rows - 3 * top_count), (0, shard - tok_count))
    )

    spread_operands = [select, grad_back, route_pack]
    spread_outs = [shape(tok_count, shard, F32)]
    spread_outs += [shape(tok_count + pack_rows, shard)] * (EXP_DEV - 1)
    grad_tokens, *pieces = call(
        spread_body, scalars, (1,), spread_operands, [whole(x) for x in spread_operands],
        spread_outs, [whole(x) for x in spread_outs], 2 * tok_count * slots * half,
        near=(select, grad_back, route_pack),
    )
    pieces = [shift(pieces[r - 1], halves * r, lanes) for r in range(1, EXP_DEV)]
    mixed, pieces[-1] = lax.optimization_barrier((mixed, pieces[-1]))
    for piece in pieces:
        piece = piece.astype(F32)
        grad_tokens = grad_tokens + piece[:tok_count]
        got = piece[tok_count:, :tok_count]
        route_sum = route_sum + (
            got[:top_count] + got[top_count : 2 * top_count] + got[2 * top_count : 3 * top_count]
        )
    grad_tokens = grad_tokens.astype(BF16)
    grad_route = route_sum.T
    return (mixed, grad_tokens, grad_route, grad_gate, grad_up, grad_down)


def solution(mesh):
    placed = (
        P("expert", "etp"),
        P("expert", None),
        P("expert", None),
        P(("expert", "etp"), None, None),
        P(("expert", "etp"), None, None),
        P(("expert", "etp"), None, None),
        P("expert", "etp"),
    )
    return jax.shard_map(
        per_device,
        mesh=mesh,
        in_specs=placed,
        out_specs=(
            P("expert", "etp"),
            P("expert", "etp"),
            P("expert", None),
            P(("expert", "etp"), None, None),
            P(("expert", "etp"), None, None),
            P(("expert", "etp"), None, None),
        ),
        check_vma=False,
    )
```

```python
import functools

import jax
import jax.numpy as jnp
from jax import lax
from jax.experimental import pallas as pl
from jax.experimental.pallas import tpu as pltpu
from jax.sharding import PartitionSpec as P

EXP_DEV = 4
ROW_CUTS = 2
SWAP_CUTS = 3
VMEM_BYTES = 28 * 1024 * 1024
F32 = jnp.float32
BF16 = jnp.bfloat16
LAST = ((1,), (1,))
FLAT = ((1,), (0,))
TALL = ((0,), (0,))


def shift(value, step, lanes):
    return lax.ppermute(value, "etp", [(i, (i + step) % lanes) for i in range(lanes)])


def swap(value, lanes):
    return lax.ppermute(value, "etp", [(i, i ^ 1) for i in range(lanes)])


def dot(a, b, dims):
    return lax.dot_general(a, b, (dims, ((), ())), preferred_element_type=F32)


def across(rows, groups):
    slots, width = rows.shape
    cut = rows.reshape(groups, slots // groups, width)
    moved = lax.all_to_all(cut, "expert", split_axis=0, concat_axis=0, tiled=True)
    return moved.reshape(slots, width)


def in_hbm(operand):
    return pltpu.with_memory_space_constraint(operand, pltpu.HBM)


def call(body, scalars, grid, operands, in_blocks, outs, out_blocks, flops, aliases=None, near=()):
    def spec(block):
        return block[0] if len(block) == 1 else pl.BlockSpec(*block)

    operands = [x if any(x is n for n in near) else in_hbm(x) for x in operands]
    return pl.pallas_call(
        body,
        grid_spec=pltpu.PrefetchScalarGridSpec(
            num_scalar_prefetch=1,
            grid=grid,
            in_specs=[spec(b) for b in in_blocks],
            out_specs=[spec(b) for b in out_blocks],
        ),
        out_shape=[pltpu.HBM(x.shape, x.dtype) for x in outs],
        input_output_aliases=aliases or {},
        compiler_params=pltpu.CompilerParams(vmem_limit_bytes=VMEM_BYTES),
        cost_estimate=pl.CostEstimate(flops=1, bytes_accessed=1, transcendentals=0),
    )(scalars, *operands)


def whole(array):
    return (array.shape, lambda i, s: (0,) * array.ndim)


def columns(parity_of, matrix, shard, halves=2):
    rows = matrix.shape[0]
    blocks = [
        ((rows, shard), lambda i, s, j=j: (0, halves * j + parity_of(s))) for j in range(EXP_DEV)
    ]
    return [matrix] * EXP_DEV, blocks


def mine_of(s):
    return lax.rem(s[0], 2)


def other_of(s):
    return 1 - lax.rem(s[0], 2)


def contract(rows_ref, w_refs):
    shard = w_refs[0].shape[1]
    parts = [
        dot(rows_ref[:, j * shard : (j + 1) * shard], w_ref[...], LAST)
        for j, w_ref in enumerate(w_refs)
    ]
    return sum(parts[1:], parts[0])


def gather_body(shard, s_ref, select_ref, *refs):
    out_ref = refs[-1]
    local_expert = s_ref[0] // 2
    select = select_ref[...]
    for r, ref in enumerate(refs[:-1]):
        start = pl.multiple_of(lax.rem(local_expert - r + EXP_DEV, EXP_DEV) * shard, shard)
        out_ref[:, pl.ds(start, shard)] = dot(select, ref[...], TALL).astype(BF16)


def scaled_body(s_ref, select_ref, grad_ref, weight_ref, out_ref):
    out_ref[...] = (dot(select_ref[...], grad_ref[...], TALL) * weight_ref[...]).astype(BF16)


def first_body(s_ref, rows_ref, *refs):
    gate_out, up_out = refs[-2:]
    gate_out[...] = contract(rows_ref, refs[:EXP_DEV])
    up_out[...] = contract(rows_ref, refs[EXP_DEV:-2])


def second_body(s_ref, rows_ref, gate_in, up_in, down_ref, *refs):
    hidden_out, gate_slope, up_slope, part_out = refs[-4:]
    gate_act = gate_in[...] + contract(rows_ref, refs[:EXP_DEV])
    up_act = up_in[...] + contract(rows_ref, refs[EXP_DEV : 2 * EXP_DEV])
    sig = jax.nn.sigmoid(gate_act)
    gated = gate_act * sig
    hidden = (gated * up_act).astype(BF16)
    hidden_out[...] = hidden
    up_slope[...] = gated
    gate_slope[...] = up_act * sig * (1.0 + gate_act * (1.0 - sig))
    part_out[...] = dot(hidden, down_ref[...], FLAT).astype(BF16)


def third_body(s_ref, grad_ref, gate_slope, up_slope, down_ref, *refs):
    gate_out, up_out, other_out = refs[-3:]
    grad_hidden = dot(grad_ref[...], down_ref[...], LAST)
    grad_gate = (grad_hidden * gate_slope[...]).astype(BF16)
    grad_up = (grad_hidden * up_slope[...]).astype(BF16)
    gate_out[...] = grad_gate
    up_out[...] = grad_up
    shard = refs[0].shape[1]
    for j in range(EXP_DEV):
        other_out[:, j * shard : (j + 1) * shard] = (
            dot(grad_gate, refs[j][...], FLAT) + dot(grad_up, refs[EXP_DEV + j][...], FLAT)
        ).astype(BF16)


def fourth_body(s_ref, grad_gate, grad_up, swapped, *refs):
    out_ref = refs[-1]
    shard = refs[0].shape[1]
    for j in range(EXP_DEV):
        here = slice(j * shard, (j + 1) * shard)
        out_ref[:, here] = (
            dot(grad_gate[...], refs[j][...], FLAT)
            + dot(grad_up[...], refs[EXP_DEV + j][...], FLAT)
            + swapped[:, here].astype(F32)
        ).astype(BF16)


def weights_body(s_ref, *refs):
    mine_ref, grad_ref, gate_out, up_out, down_out = refs[-5:]
    cuts = (len(refs) - 5) // 4
    grad_gate, grad_up, hidden, other = (refs[i * cuts : (i + 1) * cuts] for i in range(4))
    size = hidden[0].shape[0]

    def total(lefts, rights):
        parts = [dot(left[...], right, TALL) for left, right in zip(lefts, rights)]
        return sum(parts[1:], parts[0]).astype(BF16)

    def split(ref):
        return [ref[k * size : (k + 1) * size, :] for k in range(cuts)]

    down_out[0] = total(hidden, split(grad_ref))
    here = lax.rem(pl.program_id(0), 2) == lax.rem(s_ref[0], 2)

    @pl.when(here)
    def _():
        rows = split(mine_ref)
        gate_out[0] = total(grad_gate, rows)
        up_out[0] = total(grad_up, rows)

    @pl.when(jnp.logical_not(here))
    def _():
        rows = [ref[...] for ref in other]
        gate_out[0] = total(grad_gate, rows)
        up_out[0] = total(grad_up, rows)


def mix_body(s_ref, weight_ref, rows_ref, out_ref):
    both = dot(weight_ref[...], rows_ref[...], FLAT)
    tok_count = both.shape[0] // 2
    out_ref[...] = both[:tok_count] + both[tok_count:]


def route_body(s_ref, rows_ref, grad_ref, picked_ref, ids_ref, expert_ref, route_out):
    products = dot(rows_ref[...], grad_ref[...], LAST) * picked_ref[...].astype(F32)
    experts = expert_ref[...]
    for k in range(route_out.shape[0]):
        chosen = jnp.where(ids_ref[k : k + 1, :] == experts, products, 0.0)
        route_out[k : k + 1, :] = jnp.sum(chosen, axis=0, keepdims=True)


def spread_body(s_ref, select_ref, rows_ref, pack_ref, mine_out, *outs):
    count, shard = len(outs) + 1, outs[0].shape[1]
    select = select_ref[...]
    tok_count = select.shape[0]
    for r in range(count):
        start = pl.multiple_of(lax.rem(s_ref[0] // 2 + r, count) * shard, shard)
        part = dot(select, rows_ref[:, pl.ds(start, shard)], FLAT)
        if r == 0:
            mine_out[...] = part
        else:
            outs[r - 1][:tok_count, :] = part.astype(BF16)
            outs[r - 1][tok_count:, :] = pack_ref[...]


def per_device(tokens, expert_ids, route_weights, gate_weight, up_weight, down_weight, grad_out):
    tok_count, top_count = expert_ids.shape
    units, model_width = gate_weight.shape[1:]
    shard = tokens.shape[1]
    groups = lax.axis_size("expert")
    lanes = lax.axis_size("etp")
    halves = lanes // EXP_DEV
    experts = EXP_DEV * groups
    capacity = max(2, tok_count * top_count * 3 // (2 * experts))
    slots = groups * capacity
    half = model_width // halves
    lane = lax.axis_index("etp")
    local_expert = lane // halves
    scalars = lane.astype(jnp.int32).reshape(1)
    w_gate = gate_weight[0]
    w_up = up_weight[0]
    w_down = down_weight[0]
    block = slots // ROW_CUTS
    unit_flops = 2 * slots * units * half

    def shape(rows, width, kind=BF16):
        return jax.ShapeDtypeStruct((rows, width), kind)

    def row_block(width, k=None):
        return ((block, width), lambda i, s: (i if k is None else k, 0))

    grad_full = lax.all_gather(grad_out, "etp", axis=1, tiled=True)
    own = [tokens] + [shift(tokens, halves * r, lanes) for r in range(1, EXP_DEV)]

    column = lax.broadcasted_iota(jnp.int32, (1, slots), 1)
    col_expert = column // capacity * EXP_DEV + local_expert
    col_slot = (column % capacity).astype(F32)
    hits = [expert_ids[:, k : k + 1] == col_expert for k in range(top_count)]
    member = hits[0]
    for hit in hits[1:]:
        member = member | hit
    member = member.astype(BF16)
    row = lax.broadcasted_iota(jnp.int32, (tok_count, tok_count), 0)
    earlier = (lax.broadcasted_iota(jnp.int32, (tok_count, tok_count), 1) < row).astype(BF16)
    rank = dot(earlier, member, FLAT)
    chosen = (member > 0) & (rank == col_slot)
    select = chosen.astype(BF16)
    weight = jnp.zeros((tok_count, slots), F32)
    for k in range(top_count):
        weight = jnp.where(hits[k], route_weights[:, k : k + 1], weight)
    weight = jnp.where(chosen, weight, 0.0)
    slot_weight = jnp.sum(weight, axis=0)[:, None]
    weight_high = lax.reduce_precision(weight, 8, 7)
    weight_low = (weight - weight_high).astype(BF16)
    weight_high = weight_high.astype(BF16)

    (sent,) = call(
        functools.partial(gather_body, shard), scalars, (1,),
        [select, *own], [whole(select)] + [whole(x) for x in own],
        [shape(slots, half)], [((slots, half), lambda i, s: (0, 0))],
        2 * slots * tok_count * half,
        near=(select, *own),
    )
    rows_mine = across(sent, groups)
    size = slots // SWAP_CUTS
    rows_other = [swap(rows_mine[k * size : (k + 1) * size], lanes) for k in range(SWAP_CUTS)]

    (scaled,) = call(
        scaled_body, scalars, (ROW_CUTS,),
        [select, grad_full, slot_weight],
        [((tok_count, block), lambda i, s: (0, i)), whole(grad_full), row_block(1)],
        [shape(slots, model_width)], [row_block(model_width)],
        2 * slots * tok_count * model_width,
    )
    grad_rows = across(scaled, groups)

    f32_rows = shape(slots, units, F32)
    unit_block = row_block(units)
    gate_mine, mine_blocks = columns(mine_of, w_gate, shard)
    gate_other, other_blocks = columns(other_of, w_gate, shard)
    weights_mine = gate_mine + [w_up] * EXP_DEV
    weights_other = gate_other + [w_up] * EXP_DEV
    mine_blocks, other_blocks = mine_blocks * 2, other_blocks * 2
    gate_first, up_first = call(
        first_body, scalars, (ROW_CUTS,),
        [rows_mine, *weights_mine], [row_block(half)] + mine_blocks,
        [f32_rows, f32_rows], [unit_block, unit_block], 2 * unit_flops,
        near=(w_gate, w_up, w_down, rows_mine),
    )

    cut_units = shape(size, units)
    cut_wide = shape(size, units, F32)
    cut_half = shape(size, half)

    def cut_block(width, k):
        return ((size, width), lambda i, s: (k, 0))

    def placed(operands, blocks, array, position):
        if array is None:
            return None
        operands.append(array)
        blocks.append((pl.BlockSpec(memory_space=pl.ANY),))
        return {len(operands): position}

    hidden, slopes, expert_part = [], [], None
    for k in range(SWAP_CUTS):
        operands = [rows_other[k], gate_first, up_first, w_down, *weights_other]
        blocks = [whole(cut_half), cut_block(units, k), cut_block(units, k), whole(w_down)]
        blocks = blocks + other_blocks
        aliases = placed(operands, blocks, expert_part, 3)
        got = call(
            second_body, scalars, (1,), operands, blocks,
            [cut_units, cut_wide, cut_wide, shape(slots, model_width)],
            [whole(cut_units), whole(cut_wide), whole(cut_wide), cut_block(model_width, k)],
            4 * unit_flops // SWAP_CUTS, aliases,
            near=(w_gate, w_up, w_down, rows_other[k]),
        )
        hidden.append(got[0])
        slopes.append(got[1:3])
        expert_part = got[3]

    grad_gate_act, grad_up_act, swapped = [], [], []
    for k in range(SWAP_CUTS):
        got = call(
            third_body, scalars, (1,),
            [grad_rows, *slopes[k], w_down, *weights_other],
            [cut_block(model_width, k), whole(cut_wide), whole(cut_wide), whole(w_down)]
            + other_blocks,
            [cut_units, cut_units, cut_half],
            [whole(cut_units), whole(cut_units), whole(cut_half)],
            4 * unit_flops // SWAP_CUTS,
            near=(w_gate, w_up),
        )
        grad_gate_act.append(got[0])
        grad_up_act.append(got[1])
        swapped.append(swap(got[2], lanes))
    returned = across(expert_part, groups)

    pair_block = ((slots, shard), lambda i, s: (0, i // 2))
    pair_cut = ((size, shard), lambda i, s: (0, i // 2))
    grad_shape = jax.ShapeDtypeStruct((1, units, model_width), BF16)
    grad_block = ((1, units, shard), lambda i, s: (0, 0, i))
    grad_gate, grad_up, grad_down = call(
        weights_body, scalars, (lanes,),
        [*grad_gate_act, *grad_up_act, *hidden, *rows_other, rows_mine, grad_rows],
        [whole(cut_units)] * (3 * SWAP_CUTS) + [pair_cut] * SWAP_CUTS
        + [pair_block, ((slots, shard), lambda i, s: (0, i))],
        [grad_shape] * 3, [grad_block] * 3, 6 * unit_flops,
        near=(rows_mine, *rows_other),
    )

    input_half = []
    for k in range(SWAP_CUTS):
        if k == SWAP_CUTS - 1:
            returned, input_half, grad_gate, grad_up, grad_down = lax.optimization_barrier(
                (returned, input_half, grad_gate, grad_up, grad_down)
            )
            both_weights = jnp.concatenate([weight_high, weight_low], axis=0)
            (mixed_part,) = call(
                mix_body, scalars, (halves,), [both_weights, returned],
                [whole(both_weights), ((slots, half), lambda i, s: (0, i))],
                [shape(tok_count, model_width, F32)],
                [((tok_count, half), lambda i, s: (0, i))],
                4 * tok_count * slots * model_width,
            )
            swapped[k], mixed_part = lax.optimization_barrier((swapped[k], mixed_part))
        operands = [grad_gate_act[k], grad_up_act[k], swapped[k], *weights_mine]
        blocks = [whole(cut_units), whole(cut_units), whole(cut_half)] + mine_blocks
        outs, out_blocks, aliases = shape(slots, half), cut_block(half, k), None
        if k > 0:
            aliases = {len(operands) + 1: 0}
            operands.append(input_half)
            blocks.append((pl.BlockSpec(memory_space=pl.ANY),))
        (input_half,) = call(
            fourth_body, scalars, (1,), operands, blocks,
            [outs], [out_blocks], 2 * unit_flops // SWAP_CUTS, aliases,
            near=(w_gate, w_up, w_down, swapped[k]),
        )
    input_half, returned, grad_gate, grad_up, grad_down = lax.optimization_barrier(
        (input_half, returned, grad_gate, grad_up, grad_down)
    )
    grad_back = across(input_half, groups)

    picked = select.T
    ids = expert_ids.T
    row_expert = col_expert.reshape(slots, 1)
    mixed = lax.psum_scatter(mixed_part, "etp", scatter_dimension=1, tiled=True).astype(BF16)
    route_operands = [returned, grad_full, picked, ids, row_expert]
    (route_sum,) = call(
        route_body, scalars, (1,), route_operands, [whole(x) for x in route_operands],
        [shape(top_count, tok_count, F32)], [whole(ids)],
        2 * tok_count * slots * model_width,
    )
    route_sum = route_sum + swap(route_sum, lanes)
    route_1 = lax.reduce_precision(route_sum, 8, 7)
    rest = route_sum - route_1
    route_2 = lax.reduce_precision(rest, 8, 7)
    route_3 = rest - route_2
    route_pack = jnp.concatenate([route_1, route_2, route_3], axis=0).astype(BF16)
    pack_rows = -(-3 * top_count // 16) * 16
    route_pack = jnp.pad(
        route_pack, ((0, pack_rows - 3 * top_count), (0, shard - tok_count))
    )

    spread_operands = [select, grad_back, route_pack]
    spread_outs = [shape(tok_count, shard, F32)]
    spread_outs += [shape(tok_count + pack_rows, shard)] * (EXP_DEV - 1)
    grad_tokens, *pieces = call(
        spread_body, scalars, (1,), spread_operands, [whole(x) for x in spread_operands],
        spread_outs, [whole(x) for x in spread_outs], 2 * tok_count * slots * half,
        near=(select, grad_back, route_pack),
    )
    pieces = [shift(pieces[r - 1], halves * r, lanes) for r in range(1, EXP_DEV)]
    mixed, pieces[-1] = lax.optimization_barrier((mixed, pieces[-1]))
    for piece in pieces:
        piece = piece.astype(F32)
        grad_tokens = grad_tokens + piece[:tok_count]
        got = piece[tok_count:, :tok_count]
        route_sum = route_sum + (
            got[:top_count] + got[top_count : 2 * top_count] + got[2 * top_count : 3 * top_count]
        )
    grad_tokens = grad_tokens.astype(BF16)
    grad_route = route_sum.T
    return (mixed, grad_tokens, grad_route, grad_gate, grad_up, grad_down)


def solution(mesh):
    placed = (
        P("expert", "etp"),
        P("expert", None),
        P("expert", None),
        P(("expert", "etp"), None, None),
        P(("expert", "etp"), None, None),
        P(("expert", "etp"), None, None),
        P("expert", "etp"),
    )
    return jax.shard_map(
        per_device,
        mesh=mesh,
        in_specs=placed,
        out_specs=(
            P("expert", "etp"),
            P("expert", "etp"),
            P("expert", None),
            P(("expert", "etp"), None, None),
            P(("expert", "etp"), None, None),
            P(("expert", "etp"), None, None),
        ),
        check_vma=False,
    )
```
